512 devices in a mesh: gx: 16 (over z_lo, core), gy: 32 (over z_hi, y, x).
Axes of the slice: x: 4, y: 4, z: 16 (z_hi: 2, z_lo: 8; z = z_hi * 8 + z_lo), core: 2. Of those that a mesh axis runs over, the one named last changes fastest.
Arguments:
- populations: float32 [19, 256, 512, 128], P(None, 'gx', 'gy'), may hold values from 0 to 1, as said below
- seed_cells: int32 [16, 32, 128], P('gx', 'gy'), may hold values from 0 to 32767
Outputs:
- populations_out: float32 [19, 256, 512, 128], P(None, 'gx', 'gy')
- gradient: float32 [9, 16, 32, 128], P(None, 'gx', 'gy')
- q_value: float32 [16, 32, 128], P('gx', 'gy')
- r_value: float32 [16, 32, 128], P('gx', 'gy')
- vortex_share: float32 [16, 32, 128], P('gx', 'gy')
The draws below stay inside these ranges and needn't reach their ends.
Inputs may be any that keep to these rules, and one draw needn't show every extreme that they name: `populations`: every population is positive, near its equilibrium for a cell's density and flow.
All inputs are finite; a program needn't handle non-finite values.
Results may differ from the reference program's by a relative error of at most 0.000054.
Values sent between devices are 32-bit elements; how exact they have to be, the bound alone decides.
No kernel may reach another device: no remote copies, remote signals or barrier semaphores. Data moves between devices by JAX's collectives and lax.ppermute only.
A program may use at most 64 MiB of HBM per device.

```python
import jax
import jax.numpy as jnp

BX = 16
BY = 16
NZ = 128
SEEDS = 128
NX = 256
NY = 512
BLOCKS_X = 16
BLOCKS_Y = 32
N_GX = 16
N_GY = 32


DRAW_VELOCITIES = [(0, 0, 0), (1, 0, 0), (-1, 0, 0), (0, 1, 0), (0, -1, 0), (0, 0, 1), (0, 0, -1), (1, 1, 0), (-1, -1, 0), (1, -1, 0), (-1, 1, 0), (1, 0, 1), (-1, 0, -1), (1, 0, -1), (-1, 0, 1), (0, 1, 1), (0, -1, -1), (0, 1, -1), (0, -1, 1)]


DRAW_WEIGHTS = [1.0 / 3.0] + [1.0 / 18.0] * 6 + [1.0 / 36.0] * 12


def draw_populations(key, part):
    key = jax.random.fold_in(key, 11)
    key_dens, key_flow, key_noise = jax.random.split(key, 3)
    grid_shape = (NX, NY, NZ)
    density = 1.0 + 0.05 * jnp.clip(jax.random.normal(key_dens, grid_shape, jnp.float32), -3.0, 3.0)
    flows = 0.06 * jnp.clip(jax.random.normal(key_flow, (3,) + grid_shape, jnp.float32), -2.5, 2.5)
    noise = 0.1 * jnp.clip(jax.random.normal(key_noise, (19,) + grid_shape, jnp.float32), -2.5, 2.5)
    speed_sq = flows[0] * flows[0] + flows[1] * flows[1] + flows[2] * flows[2]
    result = []
    for index in range(19):
        along = DRAW_VELOCITIES[index][0] * flows[0] + DRAW_VELOCITIES[index][1] * flows[1] + DRAW_VELOCITIES[index][2] * flows[2]
        equil = DRAW_WEIGHTS[index] * density * (1.0 + 3.0 * along + 4.5 * along * along - 1.5 * speed_sq)
        result.append(equil * (1.0 + noise[index]))
    return jnp.stack(result).astype(jnp.float32)


def with_ends(values, key, low, top_value):
    longest = values.shape.index(max(values.shape))
    spots = []
    for shift in (0, 1):
        where = [jax.random.randint(jax.random.fold_in(key, axis), (), 0, length) for axis, length in enumerate(values.shape)]
        where[longest] = (where[longest] + shift) % values.shape[longest]
        spots.append(tuple(where))
    return values.at[spots[0]].set(low).at[spots[1]].set(top_value)


def setup_inputs(seed: int = 0) -> dict:
    arg_keys = jax.random.split(jax.random.key(seed), 3)
    return {
        "populations": draw_populations(jax.random.fold_in(arg_keys[2], 71), 0),
        "seed_cells": with_ends(jax.random.randint(arg_keys[1], (BLOCKS_X, BLOCKS_Y, SEEDS), 0, BX * BY * NZ), jax.random.fold_in(arg_keys[1], 1), 0, (BX * BY * NZ) - 1).astype(jnp.int32),
    }


VELOCITIES = [(0, 0, 0), (1, 0, 0), (-1, 0, 0), (0, 1, 0), (0, -1, 0), (0, 0, 1), (0, 0, -1),
              (1, 1, 0), (-1, -1, 0), (1, -1, 0), (-1, 1, 0), (1, 0, 1), (-1, 0, -1), (1, 0, -1),
              (-1, 0, 1), (0, 1, 1), (0, -1, -1), (0, 1, -1), (0, -1, 1)]
WEIGHTS = [1.0 / 3.0] + [1.0 / 18.0] * 6 + [1.0 / 36.0] * 12
RELAX_RATE = 1.6
DIFF_SCALE = 10.0


def velocity(pops):
    density = pops[0]
    for index in range(1, 19):
        density = density + pops[index]
    flows = []
    for axis_number in range(3):
        total = jnp.zeros_like(density)
        for index in range(19):
            weight = VELOCITIES[index][axis_number]
            if weight == 1:
                total = total + pops[index]
            elif weight == -1:
                total = total - pops[index]
        flows.append(total / density)
    return density, flows


def collide(pops):
    density, flows = velocity(pops)
    speed_sq = flows[0] * flows[0] + flows[1] * flows[1] + flows[2] * flows[2]
    relaxed = []
    for index in range(19):
        along = (VELOCITIES[index][0] * flows[0] + VELOCITIES[index][1] * flows[1]
                 + VELOCITIES[index][2] * flows[2])
        equil = WEIGHTS[index] * density * (1.0 + 3.0 * along + 4.5 * along * along - 1.5 * speed_sq)
        relaxed.append(pops[index] - RELAX_RATE * (pops[index] - equil))
    return relaxed


def invariants(comps):
    q_sum = jnp.zeros_like(comps[0])
    for row in range(3):
        for col in range(3):
            q_sum = q_sum + comps[3 * row + col] * comps[3 * col + row]
    r_sum = jnp.zeros_like(comps[0])
    for row in range(3):
        for col in range(3):
            for third in range(3):
                r_sum = r_sum + comps[3 * row + col] * comps[3 * col + third] * comps[3 * third + row]
    norm_sq = jnp.zeros_like(comps[0])
    for index in range(9):
        norm_sq = norm_sq + comps[index] * comps[index]
    q_value = -0.5 * q_sum
    r_value = -(1.0 / 3.0) * r_sum
    share = 2.0 * q_value / (norm_sq + 0.25)
    return q_value, r_value, share


def reference(populations, seed_cells):
    current = populations
    for repeat in range(2):
        relaxed = collide(current)
        moved = [jnp.roll(relaxed[index], VELOCITIES[index], axis=(0, 1, 2)) for index in range(19)]
        current = jnp.stack(moved)
    density, flows = velocity(current)
    comps = []
    for row in range(3):
        field = flows[row]
        comps.append((jnp.roll(field, -1, 0) - jnp.roll(field, 1, 0)) * DIFF_SCALE)
        comps.append((jnp.roll(field, -1, 1) - jnp.roll(field, 1, 1)) * DIFF_SCALE)
        comps.append((jnp.roll(field, -1, 2) - jnp.roll(field, 1, 2)) * DIFF_SCALE)
    tensor = jnp.stack(comps)
    blocks = tensor.reshape(9, N_GX, BX, N_GY, BY, NZ).transpose(0, 1, 3, 2, 4, 5)
    blocks = blocks.reshape(9, N_GX, N_GY, BX * BY * NZ)
    picked = jnp.take_along_axis(blocks, jnp.broadcast_to(seed_cells[None], (9,) + seed_cells.shape), axis=3)
    q_value, r_value, share = invariants([picked[index] for index in range(9)])
    return current, picked, q_value, r_value, share
```

```python
import jax
import jax.numpy as jnp
from jax import lax
from jax.experimental import pallas as pl
from jax.experimental.pallas import tpu as pltpu
from jax.sharding import PartitionSpec as P

C = [
    (0, 0, 0),
    (1, 0, 0),
    (-1, 0, 0),
    (0, 1, 0),
    (0, -1, 0),
    (0, 0, 1),
    (0, 0, -1),
    (1, 1, 0),
    (-1, -1, 0),
    (1, -1, 0),
    (-1, 1, 0),
    (1, 0, 1),
    (-1, 0, -1),
    (1, 0, -1),
    (-1, 0, 1),
    (0, 1, 1),
    (0, -1, -1),
    (0, 1, -1),
    (0, -1, 1),
]
W = [1.0 / 3.0] + [1.0 / 18.0] * 6 + [1.0 / 36.0] * 12
RATE = 1.6
KEEP = 1.0 - RATE
SCALE = 10.0
ALL = list(range(19))
PAIRS = [(1, 2), (3, 4), (5, 6), (7, 8), (9, 10), (11, 12), (13, 14), (15, 16), (17, 18)]
N = 16
NZ = 128
SEEDS = 128
F32 = jnp.float32
BF16 = jnp.bfloat16
ROWS = {0: (0, 1, 2), 1: (15, 14, 13)}
OWN_ROWS = (0, 1, 2, 13, 14, 15)
T_AT = 10
T_LEN = 40
WIDE = 24
YW = 20
N_A = 5
S_OFF = 13 * YW
Y_LEN = S_OFF + 4 * N
PAD_LEN = 336
V_ROWS = (-1, 0, 1, 14, 15, 16)
VMEM_LIMIT = 48 * 1024 * 1024


def x_fields(direction):
    out = [(0, i) for i in ALL]
    out += [(1, i) for i in ALL if C[i][0] != -direction]
    out += [(2, i) for i in ALL if C[i][0] == direction]
    return out


X_POS = {d: {key: k for k, key in enumerate(x_fields(d))} for d in (-1, 1)}
X_LEN = len(X_POS[1])


def zroll(v, shift):
    shift = shift % NZ
    return pltpu.roll(v, shift, axis=v.ndim - 1) if shift else v


def add_up(terms):
    terms = list(terms)
    while len(terms) > 1:
        terms = [a + b for a, b in zip(terms[::2], terms[1::2])] + (
            [terms[-1]] if len(terms) % 2 else []
        )
    return terms[0]


def moment(f, axis, indices=ALL):
    plus = [f[i] for i in indices if C[i][axis] == 1]
    minus = [f[i] for i in indices if C[i][axis] == -1]
    if plus and minus:
        return add_up(plus) - add_up(minus)
    if plus:
        return add_up(plus)
    return -add_up(minus)


def moments(f, indices=ALL):
    return [add_up(f[i] for i in indices)] + [moment(f, axis, indices) for axis in range(3)]


def equil(mom, wanted):
    rho = mom[0]
    inv = 1.0 / rho
    u = [m * inv for m in mom[1:]]
    base = 1.0 - 1.5 * (u[0] * u[0] + u[1] * u[1] + u[2] * u[2])
    r18 = rho * (RATE / 18.0)
    r36 = rho * (RATE / 36.0)
    out = {}
    if 0 in wanted:
        out[0] = rho * (RATE / 3.0) * base
    for a, b in PAIRS:
        if a not in wanted and b not in wanted:
            continue
        along = None
        for axis in range(3):
            c = C[a][axis]
            if c:
                term = u[axis] if c == 1 else -u[axis]
                along = term if along is None else along + term
        r = r18 if a < 7 else r36
        even = r * (base + 4.5 * along * along)
        odd = r * (3.0 * along)
        if a in wanted:
            out[a] = even + odd
        if b in wanted:
            out[b] = even - odd
    return out


def collide(f, wanted=ALL):
    eq = equil(moments(f), wanted)
    return {i: KEEP * f[i] + eq[i] for i in wanted}


def side_parts(s):
    toward = [i for i in ALL if C[i][1] == s]
    par = [i for i in ALL if C[i][1] == 0]
    away = [i for i in ALL if C[i][1] == -s]
    return toward, par, away


def x_pack_kernel(f_hbm, a_out, b_out, buf, sems):
    copies = [
        pltpu.make_async_copy(f_hbm.at[:, pl.ds(start, 3)], buf.at[side], sems.at[side])
        for side, start in ((0, 0), (1, N - 3))
    ]
    for copy in copies:
        copy.start()
    even = lax.rem(lax.axis_index("gx"), 2) == 0
    for side, direction in ((0, -1), (1, 1)):
        copies[side].wait()
        for layer in range(3):
            at = layer if side == 0 else 2 - layer
            wanted = [i for i in ALL if (layer, i) in X_POS[direction]]
            g = collide([buf[side, i, at] for i in ALL], wanted)

            def put(out, layer=layer, g=g, direction=direction):
                for i, value in g.items():
                    out[X_POS[direction][(layer, i)]] = value

            first = even if side == 1 else jnp.logical_not(even)
            pl.when(first)(lambda put=put: put(a_out))
            pl.when(jnp.logical_not(first))(lambda put=put: put(b_out))


def rows_kernel(f_ref, g_out):
    for r, y in enumerate(OWN_ROWS):
        g = collide([f_ref[i, pl.ds(y, N, stride=N), :] for i in ALL])
        for i in ALL:
            g_out[r, i] = g[i]


def y_pack_kernel(g_ref, xa, xb, a_out, b_out, lo, hi, t, hs):
    even_x = lax.rem(lax.axis_index("gx"), 2) == 0
    even_y = lax.rem(lax.axis_index("gy"), 2) == 0

    @pl.when(even_x)
    def _():
        hi[...] = xa[...]
        lo[...] = xb[...]

    @pl.when(jnp.logical_not(even_x))
    def _():
        hi[...] = xb[...]
        lo[...] = xa[...]

    for r, y in enumerate(OWN_ROWS):
        for i in ALL:
            t[r, i, pl.ds(T_AT, N)] = g_ref[r, i]
        for layer, i in x_fields(-1):
            t[r, i, pl.ds(T_AT + N + layer, 1)] = hi[X_POS[-1][(layer, i)], pl.ds(y, 1)]
        for layer, i in x_fields(1):
            t[r, i, pl.ds(T_AT - 1 - layer, 1)] = lo[X_POS[1][(layer, i)], pl.ds(y, 1)]

    for side, s in ((0, -1), (1, 1)):
        rows = [OWN_ROWS.index(y) for y in ROWS[side]]
        toward, par, away = side_parts(s)

        def moved(r, i, at=T_AT - 2, length=WIDE, steps=1):
            return zroll(t[r, i, pl.ds(at - steps * C[i][0], length)], steps * C[i][2])

        first = [moved(rows[0], i) for i in toward]
        beyond = {i: moved(rows[1], i) for i in toward}
        beside = {i: moved(rows[0], i) for i in par}
        both = {**beyond, **beside}
        mom = moments(both, toward + par)
        full = {i: moved(rows[0], i) for i in away}
        full.update({i: moved(rows[1], i) for i in par})
        full.update({i: moved(rows[2], i) for i in toward})
        relaxed = collide(full, toward)
        for k, i in enumerate(toward):
            hs[side, k, pl.ds(8, WIDE)] = relaxed[i]
        arrive = {
            i: zroll(hs[side, k, pl.ds(T_AT - C[i][0], N)], C[i][2]) for k, i in enumerate(toward)
        }
        for i in par:
            arrive[i] = KEEP * moved(rows[0], i, T_AT, N, 2)
        sums = moments(arrive, toward + par)
        parts = [(k * YW, v[:YW]) for k, v in enumerate(first)]
        parts += [((N_A + k) * YW, beyond[i][:YW]) for k, i in enumerate(toward)]
        parts += [((2 * N_A + k) * YW, v[:YW]) for k, v in enumerate((mom[0], mom[1], mom[3]))]
        parts += [(S_OFF + k * N, v) for k, v in enumerate(sums)]

        def put(out, parts=parts):
            for at, value in parts:
                out[pl.ds(at, value.shape[0])] = value

        to_a = even_y if side == 1 else jnp.logical_not(even_y)
        pl.when(to_a)(lambda put=put: put(a_out))
        pl.when(jnp.logical_not(to_a))(lambda put=put: put(b_out))


def seed_parts(seeds):
    zs = lax.rem(seeds, NZ)
    ys = lax.rem(lax.div(seeds, NZ), N)
    xs = lax.div(seeds, NZ * N)
    return xs, ys, zs


def one_hots(rx, ry, xs, ys):
    along_x = jnp.where(
        ry == ys, jnp.where(rx == xs + 1, 1.0, 0.0) - jnp.where(rx == xs - 1, 1.0, 0.0), 0.0
    )
    along_y = jnp.where(
        rx == xs, jnp.where(ry == ys + 1, 1.0, 0.0) - jnp.where(ry == ys - 1, 1.0, 0.0), 0.0
    )
    here = jnp.where((rx == xs) & (ry == ys), 1.0, 0.0)
    return jnp.concatenate([along_x, along_y, here], axis=1).astype(BF16)


def split3(v):
    hi = v.astype(BF16)
    rest = v - hi.astype(F32)
    mid = rest.astype(BF16)
    low = (rest - mid.astype(F32)).astype(BF16)
    return hi, mid, low


def picks(v, hots, zs):
    iz = lax.broadcasted_iota(jnp.int32, (NZ, SEEDS), 0)
    here = jnp.where(iz == zs, 1.0, 0.0)
    up = jnp.where(iz == lax.rem(zs + 1, NZ), 1.0, 0.0)
    down = jnp.where(iz == lax.rem(zs + NZ - 1, NZ), 1.0, 0.0)
    across = up - down
    out = []
    for comp in range(3):
        total = None
        for part in split3(v[comp]):
            got = lax.dot_general(
                part, hots, (((0,), (0,)), ((), ())), preferred_element_type=F32
            )
            total = got if total is None else total + got
        for kind in range(3):
            mask = across if kind == 2 else here
            piece = total[:, kind * SEEDS : (kind + 1) * SEEDS]
            out.append(jnp.sum(piece * mask, axis=0, keepdims=True))
    return out


def inside_kernel(f_ref, g_ref, xa, xb, seed_ref, f_out, fw_out, qw_out, pm_out, pick_out, hot_out, g, h, t, m, v):
    even_x = lax.rem(lax.axis_index("gx"), 2) == 0

    def halo(x_hi, x_lo):
        for layer, i in x_fields(-1):
            g[i, 3 + N + layer] = x_hi[X_POS[-1][(layer, i)]]
        for layer, i in x_fields(1):
            g[i, 2 - layer] = x_lo[X_POS[1][(layer, i)]]

    pl.when(even_x)(lambda: halo(xa, xb))
    pl.when(jnp.logical_not(even_x))(lambda: halo(xb, xa))

    def first(x, _):
        out = collide([f_ref[i, x] for i in ALL])
        for i in ALL:
            g[i, x + 3] = out[i]
        return 0

    lax.fori_loop(0, N, first, 0)
    inner = lax.broadcasted_iota(jnp.int32, (N, NZ), 0)
    inner = (inner >= 1) & (inner <= N - 2)

    def shift(value, i):
        if C[i][1]:
            value = pltpu.roll(value, C[i][1] % N, axis=0)
        return zroll(value, C[i][2])

    def second(x, _):
        f = [shift(g[i, x + 1 - C[i][0]], i) for i in ALL]
        out = collide(f)
        for i in ALL:
            h[i, x] = jnp.where(inner, out[i], 0.0)
        return 0

    lax.fori_loop(0, N + 4, second, 0)
    iy = lax.broadcasted_iota(jnp.int32, (N, NZ), 0)
    whole = (iy >= 2) & (iy <= N - 3)

    def third(x, _):
        got = [shift(h[i, x + 1 - C[i][0]], i) for i in ALL]

        @pl.when((x >= 1) & (x <= N))
        def _():
            for i in ALL:
                f_out[i, x - 1] = got[i]

        mom = moments(got)
        for k in range(4):
            m[k, pl.ds(x * N, N)] = mom[k]
        for k in range(3):
            v[k, pl.ds(x * N, N)] = jnp.where(whole, mom[k + 1] / mom[0], 0.0)
        return 0

    lax.fori_loop(0, N + 2, third, 0)
    pm_out[...] = jnp.ones_like(pm_out)
    for r, y in enumerate((0, 1, 14, 15)):
        for k in range(4):
            pm_out[r, k, pl.ds(1, N + 2)] = m[k, pl.ds(y, N + 2, stride=N), :]

    t[...] = jnp.ones_like(t)
    for r, y in enumerate(OWN_ROWS):
        if y in (2, 13):
            continue
        for i in ALL:
            t[r, i, pl.ds(T_AT, N)] = g_ref[r, i]
            for at in (-3, -2, -1, N, N + 1, N + 2):
                t[r, i, pl.ds(T_AT + at, 1)] = g[i, at + 3, pl.ds(y, 1)]
    for side, s in ((0, 1), (1, -1)):
        rows = [OWN_ROWS.index(y) for y in ROWS[side]]
        toward, par, away = side_parts(s)
        k = 0
        for r, group in ((rows[0], par), (rows[1], away)):
            for i in group:
                fw_out[side, k] = zroll(t[r, i, pl.ds(T_AT - 2 - C[i][0], WIDE)], C[i][2])
                k += 1
        leave = {
            i: zroll(t[rows[0], i, pl.ds(T_AT - 2 - C[i][0], WIDE)], C[i][2]) for i in away
        }
        for k, value in enumerate(moments(leave, away)):
            qw_out[side, k] = value

    xs, ys, zs = seed_parts(seed_ref[...])
    row = lax.broadcasted_iota(jnp.int32, ((N + 2) * N, 1), 0)
    hots = one_hots(lax.div(row, N) - 1, lax.rem(row, N), xs, ys)
    got = picks([v[k] for k in range(3)], hots, zs)
    for k in range(9):
        pick_out[pl.ds(k, 1)] = got[k]
    row = lax.broadcasted_iota(jnp.int32, (6 * WIDE, 1), 0)
    block = lax.div(row, WIDE)
    ry = jnp.where(block < 3, block - 1, block + 11)
    hot_out[...] = one_hots(lax.rem(row, WIDE) - 2, ry, xs, ys)


def outside_kernel(
    ya, yb, f_hbm, fw, qw, pm, pick, hot, seed_ref, out_hbm, grad_out, q_out, r_out, s_out, msg, hs, hp, ep, fs, sems
):
    fetch = pltpu.make_async_copy(f_hbm, fs, sems.at[0])
    fetch.start()
    even_y = lax.rem(lax.axis_index("gy"), 2) == 0

    @pl.when(even_y)
    def _():
        msg[1, pl.ds(0, Y_LEN)] = ya[...]
        msg[0, pl.ds(0, Y_LEN)] = yb[...]

    @pl.when(jnp.logical_not(even_y))
    def _():
        msg[1, pl.ds(0, Y_LEN)] = yb[...]
        msg[0, pl.ds(0, Y_LEN)] = ya[...]

    row_x = lax.broadcasted_iota(jnp.int32, (WIDE, NZ), 0) - 2
    near = (row_x >= -1) & (row_x <= N)
    own = (row_x >= 0) & (row_x < N)
    vel = {}
    patches = []
    for side, s in ((0, 1), (1, -1)):
        toward, par, away = side_parts(s)
        end, before = (0, 1) if side == 0 else (N - 1, N - 2)

        def field(k):
            return msg[side, pl.ds(k * YW, WIDE)]

        f = {i: field(k) for k, i in enumerate(toward)}
        f.update({i: fw[side, k] for k, i in enumerate(par + away)})
        out = collide(f)
        for i in ALL:
            hs[side, i, pl.ds(8, WIDE)] = out[i]
        coming = {i: field(N_A + k) for k, i in enumerate(toward)}
        mom = [
            field(2 * N_A) + qw[side, 0],
            field(2 * N_A + 1) + qw[side, 1],
            moment(coming, 1, toward) + qw[side, 2],
            field(2 * N_A + 2) + qw[side, 3],
        ]
        eq = equil(mom, toward + par)
        for k, i in enumerate(toward):
            hp[side, k, pl.ds(8, WIDE)] = KEEP * coming[i] + eq[i]
        for k, i in enumerate(par):
            ep[side, k, pl.ds(8, WIDE)] = eq[i]

        def moved(ref, k, i):
            return zroll(ref[side, k, pl.ds(8 - C[i][0], WIDE)], C[i][2])

        last = {i: moved(hp, k, i) for k, i in enumerate(toward)}
        last.update({i: moved(hs, i, i) for i in par})
        second = {i: moved(hs, i, i) for i in toward}
        for i in toward + par:
            patches.append((i, end, last[i]))
        for i in toward:
            patches.append((i, before, second[i]))
        beyond = {i: moved(hs, i, i) for i in away}
        beyond.update({i: moved(ep, k, i) for k, i in enumerate(par)})

        for y, base, terms, group, ok in (
            (end, [pm[(3 if side else 0), k] for k in range(4)], last, toward + par, near),
            (before, [pm[(2 if side else 1), k] for k in range(4)], second, toward, near),
            (
                end - s,
                [msg[side, pl.ds(S_OFF + N * k - 2, WIDE)] for k in range(4)],
                beyond,
                away + par,
                own,
            ),
        ):
            total = [a + b for a, b in zip(base, moments(terms, group))]
            inv = 1.0 / total[0]
            vel[y] = [jnp.where(ok, total[k + 1] * inv, 0.0) for k in range(3)]

    fetch.wait()
    for i, y, value in patches:
        fs[i, pl.ds(y, N, stride=N), :] = value[2 : 2 + N]
    store = pltpu.make_async_copy(fs, out_hbm, sems.at[1])
    store.start()
    zs = lax.rem(seed_ref[...], NZ)
    got = picks([jnp.concatenate([vel[y][k] for y in V_ROWS], axis=0) for k in range(3)], hot[...], zs)
    comps = [(got[k] + pick[pl.ds(k, 1)]) * SCALE for k in range(9)]
    q_sum = add_up(comps[3 * a + b] * comps[3 * b + a] for a in range(3) for b in range(3))
    r_sum = add_up(
        comps[3 * a + b] * comps[3 * b + c] * comps[3 * c + a]
        for a in range(3)
        for b in range(3)
        for c in range(3)
    )
    norm = add_up(c * c for c in comps)
    q = -0.5 * q_sum
    for k in range(9):
        grad_out[k, 0] = comps[k]
    q_out[0] = q
    r_out[0] = -(1.0 / 3.0) * r_sum
    s_out[0] = 2.0 * q / (norm + 0.25)
    store.wait()


def swaps(count):
    first = [(i, i ^ 1) for i in range(count)]
    second = []
    for i in range(1, count, 2):
        j = (i + 1) % count
        second += [(i, j), (j, i)]
    return first, second


def shape(*dims):
    return jax.ShapeDtypeStruct(dims, F32)


VM = pl.BlockSpec(memory_space=pltpu.VMEM)
ANY = pl.BlockSpec(memory_space=pl.ANY)


def params():
    return pltpu.CompilerParams(vmem_limit_bytes=VMEM_LIMIT)


def cost(flops, moved):
    return pl.CostEstimate(flops=flops, bytes_accessed=moved, transcendentals=0)


def per_device(populations, seed_cells):
    dma = pltpu.SemaphoreType.DMA
    vmem = pltpu.VMEM
    x_first, x_second = swaps(lax.axis_size("gx"))
    y_first, y_second = swaps(lax.axis_size("gy"))
    flat = populations.reshape(19, N * N, NZ)
    seeds = seed_cells.reshape(1, SEEDS)

    xa, xb = pl.pallas_call(
        x_pack_kernel,
        out_shape=[shape(X_LEN, N, NZ)] * 2,
        in_specs=[ANY],
        out_specs=[VM] * 2,
        scratch_shapes=[vmem((2, 19, 3, N, NZ), F32), dma((2,))],
        compiler_params=params(),
        cost_estimate=cost(5_000_000, 1_500_000),
        name="x_pack",
    )(populations)
    xb = lax.ppermute(xb, "gx", x_second)
    xa = lax.ppermute(xa, "gx", x_first)
    g_rows = pl.pallas_call(
        rows_kernel,
        out_shape=shape(6, 19, N, NZ),
        in_specs=[VM],
        out_specs=VM,
        compiler_params=params(),
        cost_estimate=cost(5_000_000, 3_500_000),
        name="end_rows",
    )(flat)
    ya, yb = pl.pallas_call(
        y_pack_kernel,
        out_shape=[shape(Y_LEN, NZ)] * 2,
        in_specs=[VM] * 3,
        out_specs=[VM] * 2,
        scratch_shapes=[
            vmem((X_LEN, N, NZ), F32),
            vmem((X_LEN, N, NZ), F32),
            vmem((6, 19, T_LEN, NZ), F32),
            vmem((2, N_A, T_LEN, NZ), F32),
        ],
        compiler_params=params(),
        cost_estimate=cost(5_000_000, 2_000_000),
        name="y_pack",
    )(g_rows, xa, xb)
    yb = lax.ppermute(yb, "gy", y_second)
    ya = lax.ppermute(ya, "gy", y_first)
    inside, fw, qw, pm, pick, hot = pl.pallas_call(
        inside_kernel,
        out_shape=[
            shape(19, N, N, NZ),
            shape(2, 14, WIDE, NZ),
            shape(2, 4, WIDE, NZ),
            shape(4, 4, WIDE, NZ),
            shape(9, SEEDS),
            jax.ShapeDtypeStruct((6 * WIDE, 3 * SEEDS), BF16),
        ],
        in_specs=[VM] * 5,
        out_specs=[VM] * 6,
        scratch_shapes=[
            vmem((19, N + 6, N, NZ), F32),
            vmem((19, N + 4, N, NZ), F32),
            vmem((6, 19, T_LEN, NZ), F32),
            vmem((4, (N + 2) * N, NZ), F32),
            vmem((3, (N + 2) * N, NZ), F32),
        ],
        compiler_params=params(),
        cost_estimate=cost(50_000_000, 30_000_000),
        name="inside",
    )(populations, g_rows, xa, xb, seeds)
    out, grad, q_value, r_value, share = pl.pallas_call(
        outside_kernel,
        out_shape=[shape(19, N * N, NZ), shape(9, 1, 1, SEEDS)] + [shape(1, 1, SEEDS)] * 3,
        in_specs=[VM, VM, ANY] + [VM] * 6,
        out_specs=[ANY] + [VM] * 4,
        scratch_shapes=[
            vmem((2, PAD_LEN, NZ), F32),
            vmem((2, 19, T_LEN, NZ), F32),
            vmem((2, N_A, T_LEN, NZ), F32),
            vmem((2, 9, T_LEN, NZ), F32),
            vmem((19, N * N, NZ), F32),
            dma((2,)),
        ],
        compiler_params=params(),
        cost_estimate=cost(5_000_000, 8_000_000),
        name="outside",
    )(ya, yb, inside.reshape(19, N * N, NZ), fw, qw, pm, pick, hot, seeds)
    return out.reshape(19, N, N, NZ), grad, q_value, r_value, share


def solution(mesh):
    in_specs = (P(None, "gx", "gy", None), P("gx", "gy", None))
    out_specs = (
        P(None, "gx", "gy", None),
        P(None, "gx", "gy", None),
        P("gx", "gy", None),
        P("gx", "gy", None),
        P("gx", "gy", None),
    )
    return jax.shard_map(
        per_device, mesh=mesh, in_specs=in_specs, out_specs=out_specs, check_vma=False
    )
```

```python
import jax
import jax.numpy as jnp
from jax import lax
from jax.experimental import pallas as pl
from jax.experimental.pallas import tpu as pltpu
from jax.sharding import PartitionSpec as P

C = [
    (0, 0, 0),
    (1, 0, 0),
    (-1, 0, 0),
    (0, 1, 0),
    (0, -1, 0),
    (0, 0, 1),
    (0, 0, -1),
    (1, 1, 0),
    (-1, -1, 0),
    (1, -1, 0),
    (-1, 1, 0),
    (1, 0, 1),
    (-1, 0, -1),
    (1, 0, -1),
    (-1, 0, 1),
    (0, 1, 1),
    (0, -1, -1),
    (0, 1, -1),
    (0, -1, 1),
]
W = [1.0 / 3.0] + [1.0 / 18.0] * 6 + [1.0 / 36.0] * 12
RATE = 1.6
KEEP = 1.0 - RATE
SCALE = 10.0
ALL = list(range(19))
PAIRS = [(1, 2), (3, 4), (5, 6), (7, 8), (9, 10), (11, 12), (13, 14), (15, 16), (17, 18)]
N = 16
NZ = 128
SEEDS = 128
F32 = jnp.float32
BF16 = jnp.bfloat16
ROWS = {0: (0, 1, 2), 1: (15, 14, 13)}
OWN_ROWS = (0, 1, 2, 13, 14, 15)
T_AT = 10
T_LEN = 40
WIDE = 24
YW = 20
N_A = 5
S_OFF = 13 * YW
Y_LEN = S_OFF + 4 * N
PAD_LEN = 336
V_ROWS = (-1, 0, 1, 14, 15, 16)
UNROLL = 4
VMEM_LIMIT = 28 * 1024 * 1024


def x_fields(direction):
    out = [(0, i) for i in ALL]
    out += [(1, i) for i in ALL if C[i][0] != -direction]
    out += [(2, i) for i in ALL if C[i][0] == direction]
    return out


X_POS = {d: {key: k for k, key in enumerate(x_fields(d))} for d in (-1, 1)}
X_LEN = len(X_POS[1])


def zroll(v, shift):
    shift = shift % NZ
    return pltpu.roll(v, shift, axis=v.ndim - 1) if shift else v


def add_up(terms):
    terms = list(terms)
    while len(terms) > 1:
        terms = [a + b for a, b in zip(terms[::2], terms[1::2])] + (
            [terms[-1]] if len(terms) % 2 else []
        )
    return terms[0]


def moment(f, axis, indices=ALL):
    plus = [f[i] for i in indices if C[i][axis] == 1]
    minus = [f[i] for i in indices if C[i][axis] == -1]
    if plus and minus:
        return add_up(plus) - add_up(minus)
    if plus:
        return add_up(plus)
    return -add_up(minus)


def moments(f, indices=ALL):
    return [add_up(f[i] for i in indices)] + [moment(f, axis, indices) for axis in range(3)]


def equil(mom, wanted):
    rho = mom[0]
    inv = 1.0 / rho
    u = [m * inv for m in mom[1:]]
    base = 1.0 - 1.5 * (u[0] * u[0] + u[1] * u[1] + u[2] * u[2])
    r18 = rho * (RATE / 18.0)
    r36 = rho * (RATE / 36.0)
    out = {}
    if 0 in wanted:
        out[0] = rho * (RATE / 3.0) * base
    for a, b in PAIRS:
        if a not in wanted and b not in wanted:
            continue
        along = None
        for axis in range(3):
            c = C[a][axis]
            if c:
                term = u[axis] if c == 1 else -u[axis]
                along = term if along is None else along + term
        r = r18 if a < 7 else r36
        even = r * (base + 4.5 * along * along)
        odd = r * (3.0 * along)
        if a in wanted:
            out[a] = even + odd
        if b in wanted:
            out[b] = even - odd
    return out


def collide(f, wanted=ALL):
    eq = equil(moments(f), wanted)
    return {i: KEEP * f[i] + eq[i] for i in wanted}


def side_parts(s):
    toward = [i for i in ALL if C[i][1] == s]
    par = [i for i in ALL if C[i][1] == 0]
    away = [i for i in ALL if C[i][1] == -s]
    return toward, par, away


def x_pack_kernel(f_hbm, a_out, b_out, buf, sems):
    copies = [
        pltpu.make_async_copy(f_hbm.at[:, pl.ds(start, 3)], buf.at[side], sems.at[side])
        for side, start in ((0, 0), (1, N - 3))
    ]
    for copy in copies:
        copy.start()
    even = lax.rem(lax.axis_index("gx"), 2) == 0
    for side, direction in ((0, -1), (1, 1)):
        copies[side].wait()
        for layer in range(3):
            at = layer if side == 0 else 2 - layer
            wanted = [i for i in ALL if (layer, i) in X_POS[direction]]
            g = collide([buf[side, i, at] for i in ALL], wanted)

            def put(out, layer=layer, g=g, direction=direction):
                for i, value in g.items():
                    out[X_POS[direction][(layer, i)]] = value

            first = even if side == 1 else jnp.logical_not(even)
            pl.when(first)(lambda put=put: put(a_out))
            pl.when(jnp.logical_not(first))(lambda put=put: put(b_out))


def rows_kernel(f_ref, seed_ref, g_out, inner_out, outer_out):
    for r, y in enumerate(OWN_ROWS):
        g = collide([f_ref[i, pl.ds(y, N, stride=N), :] for i in ALL])
        for i in ALL:
            g_out[r, i] = g[i]
    xs, ys, _ = seed_parts(seed_ref[...])
    row = lax.broadcasted_iota(jnp.int32, ((N + 2) * N, 1), 0)
    inner_out[...] = one_hots(lax.div(row, N) - 1, lax.rem(row, N), xs, ys)
    row = lax.broadcasted_iota(jnp.int32, (6 * WIDE, 1), 0)
    block = lax.div(row, WIDE)
    ry = jnp.where(block < 3, block - 1, block + 11)
    outer_out[...] = one_hots(lax.rem(row, WIDE) - 2, ry, xs, ys)


def y_pack_kernel(g_ref, xb, xa, a_out, b_out, t, lo, hi, hs):
    even_x = lax.rem(lax.axis_index("gx"), 2) == 0
    even_y = lax.rem(lax.axis_index("gy"), 2) == 0

    @pl.when(even_x)
    def _():
        hi[...] = xa[...]
        lo[...] = xb[...]

    @pl.when(jnp.logical_not(even_x))
    def _():
        hi[...] = xb[...]
        lo[...] = xa[...]

    for r, y in enumerate(OWN_ROWS):
        for i in ALL:
            t[r, i, pl.ds(T_AT, N)] = g_ref[r, i]
        for layer, i in x_fields(-1):
            t[r, i, pl.ds(T_AT + N + layer, 1)] = hi[X_POS[-1][(layer, i)], pl.ds(y, 1)]
        for layer, i in x_fields(1):
            t[r, i, pl.ds(T_AT - 1 - layer, 1)] = lo[X_POS[1][(layer, i)], pl.ds(y, 1)]

    for side, s in ((0, -1), (1, 1)):
        rows = [OWN_ROWS.index(y) for y in ROWS[side]]
        toward, par, away = side_parts(s)

        def moved(r, i, at=T_AT - 2, length=WIDE, steps=1):
            return zroll(t[r, i, pl.ds(at - steps * C[i][0], length)], steps * C[i][2])

        first = [moved(rows[0], i) for i in toward]
        beyond = {i: moved(rows[1], i) for i in toward}
        beside = {i: moved(rows[0], i) for i in par}
        both = {**beyond, **beside}
        mom = moments(both, toward + par)
        full = {i: moved(rows[0], i) for i in away}
        full.update({i: moved(rows[1], i) for i in par})
        full.update({i: moved(rows[2], i) for i in toward})
        relaxed = collide(full, toward)
        for k, i in enumerate(toward):
            hs[side, k, pl.ds(8, WIDE)] = relaxed[i]
        arrive = {
            i: zroll(hs[side, k, pl.ds(T_AT - C[i][0], N)], C[i][2]) for k, i in enumerate(toward)
        }
        for i in par:
            arrive[i] = KEEP * moved(rows[0], i, T_AT, N, 2)
        sums = moments(arrive, toward + par)
        parts = [(k * YW, v[:YW]) for k, v in enumerate(first)]
        parts += [((N_A + k) * YW, beyond[i][:YW]) for k, i in enumerate(toward)]
        parts += [((2 * N_A + k) * YW, v[:YW]) for k, v in enumerate((mom[0], mom[1], mom[3]))]
        parts += [(S_OFF + k * N, v) for k, v in enumerate(sums)]

        def put(out, parts=parts):
            for at, value in parts:
                out[pl.ds(at, value.shape[0])] = value

        to_a = even_y if side == 1 else jnp.logical_not(even_y)
        pl.when(to_a)(lambda put=put: put(a_out))
        pl.when(jnp.logical_not(to_a))(lambda put=put: put(b_out))


def seed_parts(seeds):
    zs = lax.rem(seeds, NZ)
    ys = lax.rem(lax.div(seeds, NZ), N)
    xs = lax.div(seeds, NZ * N)
    return xs, ys, zs


def one_hots(rx, ry, xs, ys):
    along_x = jnp.where(
        ry == ys, jnp.where(rx == xs + 1, 1.0, 0.0) - jnp.where(rx == xs - 1, 1.0, 0.0), 0.0
    )
    along_y = jnp.where(
        rx == xs, jnp.where(ry == ys + 1, 1.0, 0.0) - jnp.where(ry == ys - 1, 1.0, 0.0), 0.0
    )
    here = jnp.where((rx == xs) & (ry == ys), 1.0, 0.0)
    return jnp.concatenate([along_x, along_y, here], axis=1).astype(BF16)


def split3(v):
    hi = v.astype(BF16)
    rest = v - hi.astype(F32)
    mid = rest.astype(BF16)
    low = (rest - mid.astype(F32)).astype(BF16)
    return hi, mid, low


def picks(v, hots, zs):
    iz = lax.broadcasted_iota(jnp.int32, (NZ, SEEDS), 0)
    here = jnp.where(iz == zs, 1.0, 0.0)
    up = jnp.where(iz == lax.rem(zs + 1, NZ), 1.0, 0.0)
    down = jnp.where(iz == lax.rem(zs + NZ - 1, NZ), 1.0, 0.0)
    across = up - down
    out = []
    for comp in range(3):
        total = None
        for part in split3(v[comp]):
            got = lax.dot_general(
                part, hots, (((0,), (0,)), ((), ())), preferred_element_type=F32
            )
            total = got if total is None else total + got
        for kind in range(3):
            mask = across if kind == 2 else here
            piece = total[:, kind * SEEDS : (kind + 1) * SEEDS]
            out.append(jnp.sum(piece * mask, axis=0, keepdims=True))
    return out


def inside_kernel(f_ref, t, xa, xb, hots, seed_ref, f_out, fw_out, qw_out, pm_out, pick_out, g, h, m, v):
    even_x = lax.rem(lax.axis_index("gx"), 2) == 0

    def halo(x_hi, x_lo):
        for layer, i in x_fields(-1):
            g[i, 3 + N + layer] = x_hi[X_POS[-1][(layer, i)]]
        for layer, i in x_fields(1):
            g[i, 2 - layer] = x_lo[X_POS[1][(layer, i)]]

    pl.when(even_x)(lambda: halo(xa, xb))
    pl.when(jnp.logical_not(even_x))(lambda: halo(xb, xa))

    for side, s in ((0, 1), (1, -1)):
        rows = [OWN_ROWS.index(y) for y in ROWS[side]]
        toward, par, away = side_parts(s)
        k = 0
        for r, group in ((rows[0], par), (rows[1], away)):
            for i in group:
                fw_out[side, k] = zroll(t[r, i, pl.ds(T_AT - 2 - C[i][0], WIDE)], C[i][2])
                k += 1
        leave = {
            i: zroll(t[rows[0], i, pl.ds(T_AT - 2 - C[i][0], WIDE)], C[i][2]) for i in away
        }
        for k, value in enumerate(moments(leave, away)):
            qw_out[side, k] = value

    def first(x, _):
        out = collide([f_ref[i, pl.ds(pl.multiple_of(x * N, N), N)] for i in ALL])
        for i in ALL:
            g[i, x + 3] = out[i]
        return 0

    lax.fori_loop(0, N, first, 0, unroll=UNROLL)
    inner = lax.broadcasted_iota(jnp.int32, (N, NZ), 0)
    inner = (inner >= 1) & (inner <= N - 2)

    def shift(value, i):
        if C[i][1]:
            value = pltpu.roll(value, C[i][1] % N, axis=0)
        return zroll(value, C[i][2])

    def second(x, _):
        f = [shift(g[i, x + 1 - C[i][0]], i) for i in ALL]
        out = collide(f)
        for i in ALL:
            h[i, x] = jnp.where(inner, out[i], 0.0)
        return 0

    lax.fori_loop(0, N + 4, second, 0, unroll=UNROLL)
    iy = lax.broadcasted_iota(jnp.int32, (N, NZ), 0)
    whole = (iy >= 2) & (iy <= N - 3)

    def third(x, _):
        got = [shift(h[i, x + 1 - C[i][0]], i) for i in ALL]

        @pl.when((x >= 1) & (x <= N))
        def _():
            for i in ALL:
                f_out[i, x - 1] = got[i]

        mom = moments(got)
        for k in range(4):
            m[k, pl.ds(x * N, N)] = mom[k]
        for k in range(3):
            v[k, pl.ds(x * N, N)] = jnp.where(whole, mom[k + 1] / mom[0], 0.0)
        return 0

    lax.fori_loop(0, N + 2, third, 0, unroll=UNROLL)
    pm_out[...] = jnp.ones_like(pm_out)
    for r, y in enumerate((0, 1, 14, 15)):
        for k in range(4):
            pm_out[r, k, pl.ds(1, N + 2)] = m[k, pl.ds(y, N + 2, stride=N), :]

    zs = lax.rem(seed_ref[...], NZ)
    got = picks([v[k] for k in range(3)], hots[...], zs)
    for k in range(9):
        pick_out[pl.ds(k, 1)] = got[k]


def outside_kernel(
    yb, ya, f_in, fw, qw, pm, pick, hot, seed_ref, out_hbm, grad_out, q_out, r_out, s_out, msg, hs, hp, ep, fs, sems
):
    even_y = lax.rem(lax.axis_index("gy"), 2) == 0

    @pl.when(even_y)
    def _():
        msg[1, pl.ds(0, Y_LEN)] = ya[...]
        msg[0, pl.ds(0, Y_LEN)] = yb[...]

    @pl.when(jnp.logical_not(even_y))
    def _():
        msg[1, pl.ds(0, Y_LEN)] = yb[...]
        msg[0, pl.ds(0, Y_LEN)] = ya[...]

    row_x = lax.broadcasted_iota(jnp.int32, (WIDE, NZ), 0) - 2
    near = (row_x >= -1) & (row_x <= N)
    own = (row_x >= 0) & (row_x < N)
    vel = {}
    patches = []
    for side, s in ((0, 1), (1, -1)):
        toward, par, away = side_parts(s)
        end, before = (0, 1) if side == 0 else (N - 1, N - 2)

        def field(k):
            return msg[side, pl.ds(k * YW, WIDE)]

        f = {i: field(k) for k, i in enumerate(toward)}
        f.update({i: fw[side, k] for k, i in enumerate(par + away)})
        out = collide(f)
        for i in ALL:
            hs[side, i, pl.ds(8, WIDE)] = out[i]
        coming = {i: field(N_A + k) for k, i in enumerate(toward)}
        mom = [
            field(2 * N_A) + qw[side, 0],
            field(2 * N_A + 1) + qw[side, 1],
            moment(coming, 1, toward) + qw[side, 2],
            field(2 * N_A + 2) + qw[side, 3],
        ]
        eq = equil(mom, toward + par)
        for k, i in enumerate(toward):
            hp[side, k, pl.ds(8, WIDE)] = KEEP * coming[i] + eq[i]
        for k, i in enumerate(par):
            ep[side, k, pl.ds(8, WIDE)] = eq[i]

        def moved(ref, k, i):
            return zroll(ref[side, k, pl.ds(8 - C[i][0], WIDE)], C[i][2])

        last = {i: moved(hp, k, i) for k, i in enumerate(toward)}
        last.update({i: moved(hs, i, i) for i in par})
        second = {i: moved(hs, i, i) for i in toward}
        for i in toward + par:
            patches.append((i, end, last[i]))
        for i in toward:
            patches.append((i, before, second[i]))
        beyond = {i: moved(hs, i, i) for i in away}
        beyond.update({i: moved(ep, k, i) for k, i in enumerate(par)})

        for y, base, terms, group, ok in (
            (end, [pm[(3 if side else 0), k] for k in range(4)], last, toward + par, near),
            (before, [pm[(2 if side else 1), k] for k in range(4)], second, toward, near),
            (
                end - s,
                [msg[side, pl.ds(S_OFF + N * k - 2, WIDE)] for k in range(4)],
                beyond,
                away + par,
                own,
            ),
        ):
            total = [a + b for a, b in zip(base, moments(terms, group))]
            inv = 1.0 / total[0]
            vel[y] = [jnp.where(ok, total[k + 1] * inv, 0.0) for k in range(3)]

    stores = []
    for i in ALL:
        fs[i] = f_in[i]
        for k, y, value in patches:
            if k == i:
                fs[i, pl.ds(y, N, stride=N), :] = value[2 : 2 + N]
        stores.append(pltpu.make_async_copy(fs.at[i], out_hbm.at[i], sems.at[i]))
        stores[-1].start()
    zs = lax.rem(seed_ref[...], NZ)
    got = picks([jnp.concatenate([vel[y][k] for y in V_ROWS], axis=0) for k in range(3)], hot[...], zs)
    comps = [(got[k] + pick[pl.ds(k, 1)]) * SCALE for k in range(9)]
    q_sum = add_up(comps[3 * a + b] * comps[3 * b + a] for a in range(3) for b in range(3))
    r_sum = add_up(
        comps[3 * a + b] * comps[3 * b + c] * comps[3 * c + a]
        for a in range(3)
        for b in range(3)
        for c in range(3)
    )
    norm = add_up(c * c for c in comps)
    q = -0.5 * q_sum
    for k in range(9):
        grad_out[k, 0] = comps[k]
    q_out[0] = q
    r_out[0] = -(1.0 / 3.0) * r_sum
    s_out[0] = 2.0 * q / (norm + 0.25)
    for store in stores:
        store.wait()


def swaps(count):
    first = [(i, i ^ 1) for i in range(count)]
    second = []
    for i in range(1, count, 2):
        j = (i + 1) % count
        second += [(i, j), (j, i)]
    return first, second


def shape(*dims):
    return jax.ShapeDtypeStruct(dims, F32)


VM = pl.BlockSpec(memory_space=pltpu.VMEM)
ANY = pl.BlockSpec(memory_space=pl.ANY)


def params():
    return pltpu.CompilerParams(vmem_limit_bytes=VMEM_LIMIT)


def cost(flops, moved):
    return pl.CostEstimate(flops=flops, bytes_accessed=moved, transcendentals=0)


def per_device(populations, seed_cells):
    dma = pltpu.SemaphoreType.DMA
    vmem = pltpu.VMEM
    x_first, x_second = swaps(lax.axis_size("gx"))
    y_first, y_second = swaps(lax.axis_size("gy"))
    flat = populations.reshape(19, N * N, NZ)
    seeds = seed_cells.reshape(1, SEEDS)

    xa, xb = pl.pallas_call(
        x_pack_kernel,
        out_shape=[shape(X_LEN, N, NZ)] * 2,
        in_specs=[ANY],
        out_specs=[VM] * 2,
        scratch_shapes=[vmem((2, 19, 3, N, NZ), F32), dma((2,))],
        compiler_params=params(),
        cost_estimate=cost(5_000_000, 1_500_000),
        name="x_pack",
    )(populations)
    xb = lax.ppermute(xb, "gx", x_second)
    xa = lax.ppermute(xa, "gx", x_first)
    g_rows, hot_in, hot = pl.pallas_call(
        rows_kernel,
        out_shape=[
            shape(6, 19, N, NZ),
            jax.ShapeDtypeStruct(((N + 2) * N, 3 * SEEDS), BF16),
            jax.ShapeDtypeStruct((6 * WIDE, 3 * SEEDS), BF16),
        ],
        in_specs=[VM] * 2,
        out_specs=[VM] * 3,
        compiler_params=params(),
        cost_estimate=cost(5_000_000, 3_500_000),
        name="end_rows",
    )(flat, seeds)
    ya, yb, t = pl.pallas_call(
        y_pack_kernel,
        out_shape=[shape(Y_LEN, NZ)] * 2 + [shape(6, 19, T_LEN, NZ)],
        in_specs=[VM] * 3,
        out_specs=[VM] * 3,
        scratch_shapes=[
            vmem((X_LEN, N, NZ), F32),
            vmem((X_LEN, N, NZ), F32),
            vmem((2, N_A, T_LEN, NZ), F32),
        ],
        compiler_params=params(),
        cost_estimate=cost(5_000_000, 2_000_000),
        name="y_pack",
    )(g_rows, xb, xa)
    yb = lax.ppermute(yb, "gy", y_second)
    ya = lax.ppermute(ya, "gy", y_first)
    inside, fw, qw, pm, pick = pl.pallas_call(
        inside_kernel,
        out_shape=[
            shape(19, N, N, NZ),
            shape(2, 14, WIDE, NZ),
            shape(2, 4, WIDE, NZ),
            shape(4, 4, WIDE, NZ),
            shape(9, SEEDS),
        ],
        in_specs=[VM] * 6,
        out_specs=[VM] * 5,
        scratch_shapes=[
            vmem((19, N + 6, N, NZ), F32),
            vmem((19, N + 4, N, NZ), F32),
            vmem((4, (N + 2) * N, NZ), F32),
            vmem((3, (N + 2) * N, NZ), F32),
        ],
        compiler_params=params(),
        cost_estimate=cost(50_000_000, 30_000_000),
        name="inside",
    )(flat, t, xa, xb, hot_in, seeds)
    out, grad, q_value, r_value, share = pl.pallas_call(
        outside_kernel,
        out_shape=[shape(19, N * N, NZ), shape(9, 1, 1, SEEDS)] + [shape(1, 1, SEEDS)] * 3,
        in_specs=[VM] * 9,
        out_specs=[ANY] + [VM] * 4,
        scratch_shapes=[
            vmem((2, PAD_LEN, NZ), F32),
            vmem((2, 19, T_LEN, NZ), F32),
            vmem((2, N_A, T_LEN, NZ), F32),
            vmem((2, 9, T_LEN, NZ), F32),
            vmem((19, N * N, NZ), F32),
            dma((19,)),
        ],
        compiler_params=params(),
        cost_estimate=cost(5_000_000, 8_000_000),
        name="outside",
    )(yb, ya, inside.reshape(19, N * N, NZ), fw, qw, pm, pick, hot, seeds)
    return out.reshape(19, N, N, NZ), grad, q_value, r_value, share


def solution(mesh):
    in_specs = (P(None, "gx", "gy", None), P("gx", "gy", None))
    out_specs = (
        P(None, "gx", "gy", None),
        P(None, "gx", "gy", None),
        P("gx", "gy", None),
        P("gx", "gy", None),
        P("gx", "gy", None),
    )
    return jax.shard_map(
        per_device, mesh=mesh, in_specs=in_specs, out_specs=out_specs, check_vma=False
    )
```

```python
import jax
import jax.numpy as jnp
from jax import lax
from jax.experimental import pallas as pl
from jax.experimental.pallas import tpu as pltpu
from jax.sharding import PartitionSpec as P

C = [
    (0, 0, 0),
    (1, 0, 0),
    (-1, 0, 0),
    (0, 1, 0),
    (0, -1, 0),
    (0, 0, 1),
    (0, 0, -1),
    (1, 1, 0),
    (-1, -1, 0),
    (1, -1, 0),
    (-1, 1, 0),
    (1, 0, 1),
    (-1, 0, -1),
    (1, 0, -1),
    (-1, 0, 1),
    (0, 1, 1),
    (0, -1, -1),
    (0, 1, -1),
    (0, -1, 1),
]
W = [1.0 / 3.0] + [1.0 / 18.0] * 6 + [1.0 / 36.0] * 12
RATE = 1.6
KEEP = 1.0 - RATE
SCALE = 10.0
ALL = list(range(19))
PAIRS = [(1, 2), (3, 4), (5, 6), (7, 8), (9, 10), (11, 12), (13, 14), (15, 16), (17, 18)]
N = 16
NZ = 128
SEEDS = 128
F32 = jnp.float32
BF16 = jnp.bfloat16
ROWS = {0: (0, 1, 2), 1: (15, 14, 13)}
OWN_ROWS = (0, 1, 2, 13, 14, 15)
T_AT = 10
T_LEN = 40
WIDE = 24
YW = 20
N_A = 5
S_OFF = 13 * YW
Y_LEN = S_OFF + 4 * N
PAD_LEN = 336
FAR_LEN = 328
V_ROWS = (-1, 0, 1, 14, 15, 16)
UNROLL = 4
VMEM_LIMIT = 28 * 1024 * 1024


def x_fields(direction):
    out = [(0, i) for i in ALL]
    out += [(1, i) for i in ALL if C[i][0] != -direction]
    out += [(2, i) for i in ALL if C[i][0] == direction]
    return out


X_POS = {d: {key: k for k, key in enumerate(x_fields(d))} for d in (-1, 1)}
X_LEN = len(X_POS[1])


def zroll(v, shift):
    shift = shift % NZ
    return pltpu.roll(v, shift, axis=v.ndim - 1) if shift else v


def add_up(terms):
    terms = list(terms)
    while len(terms) > 1:
        terms = [a + b for a, b in zip(terms[::2], terms[1::2])] + (
            [terms[-1]] if len(terms) % 2 else []
        )
    return terms[0]


def moment(f, axis, indices=ALL):
    plus = [f[i] for i in indices if C[i][axis] == 1]
    minus = [f[i] for i in indices if C[i][axis] == -1]
    if plus and minus:
        return add_up(plus) - add_up(minus)
    if plus:
        return add_up(plus)
    return -add_up(minus)


def moments(f, indices=ALL):
    return [add_up(f[i] for i in indices)] + [moment(f, axis, indices) for axis in range(3)]


def equil(mom, wanted):
    rho = mom[0]
    inv = 1.0 / rho
    u = [m * inv for m in mom[1:]]
    base = 1.0 - 1.5 * (u[0] * u[0] + u[1] * u[1] + u[2] * u[2])
    r18 = rho * (RATE / 18.0)
    r36 = rho * (RATE / 36.0)
    out = {}
    if 0 in wanted:
        out[0] = rho * (RATE / 3.0) * base
    for a, b in PAIRS:
        if a not in wanted and b not in wanted:
            continue
        along = None
        for axis in range(3):
            c = C[a][axis]
            if c:
                term = u[axis] if c == 1 else -u[axis]
                along = term if along is None else along + term
        r = r18 if a < 7 else r36
        even = r * (base + 4.5 * along * along)
        odd = r * (3.0 * along)
        if a in wanted:
            out[a] = even + odd
        if b in wanted:
            out[b] = even - odd
    return out


def collide(f, wanted=ALL):
    eq = equil(moments(f), wanted)
    return {i: KEEP * f[i] + eq[i] for i in wanted}


def side_parts(s):
    toward = [i for i in ALL if C[i][1] == s]
    par = [i for i in ALL if C[i][1] == 0]
    away = [i for i in ALL if C[i][1] == -s]
    return toward, par, away


def x_pack_kernel(f_hbm, a_out, b_out, buf, sems):
    copies = [
        pltpu.make_async_copy(f_hbm.at[:, pl.ds(start, 3)], buf.at[side], sems.at[side])
        for side, start in ((0, 0), (1, N - 3))
    ]
    for copy in copies:
        copy.start()
    even = lax.rem(lax.axis_index("gx"), 2) == 0
    for side, direction in ((0, -1), (1, 1)):
        copies[side].wait()
        for layer in range(3):
            at = layer if side == 0 else 2 - layer
            wanted = [i for i in ALL if (layer, i) in X_POS[direction]]
            g = collide([buf[side, i, at] for i in ALL], wanted)

            def put(out, layer=layer, g=g, direction=direction):
                for i, value in g.items():
                    out[X_POS[direction][(layer, i)]] = value

            first = even if side == 1 else jnp.logical_not(even)
            pl.when(first)(lambda put=put: put(a_out))
            pl.when(jnp.logical_not(first))(lambda put=put: put(b_out))


def rows_kernel(f_ref, seed_ref, g_out, inner_out, outer_out):
    for r, y in enumerate(OWN_ROWS):
        used = {2: side_parts(-1)[0], N - 3: side_parts(1)[0]}.get(y, ALL)
        g = collide([f_ref[i, pl.ds(y, N, stride=N), :] for i in ALL], used)
        for i in used:
            g_out[r, i] = g[i]
    xs, ys, _ = seed_parts(seed_ref[...])
    row = lax.broadcasted_iota(jnp.int32, ((N + 2) * N, 1), 0)
    inner_out[...] = one_hots(lax.div(row, N) - 1, lax.rem(row, N), xs, ys)
    row = lax.broadcasted_iota(jnp.int32, (6 * WIDE, 1), 0)
    block = lax.div(row, WIDE)
    ry = jnp.where(block < 3, block - 1, block + 11)
    outer_out[...] = one_hots(lax.rem(row, WIDE) - 2, ry, xs, ys)


def y_pack_kernel(g_ref, xb, xa, a_out, b_out, t, lo, hi, hs):
    even_x = lax.rem(lax.axis_index("gx"), 2) == 0
    even_y = lax.rem(lax.axis_index("gy"), 2) == 0

    @pl.when(even_x)
    def _():
        hi[...] = xa[...]
        lo[...] = xb[...]

    @pl.when(jnp.logical_not(even_x))
    def _():
        hi[...] = xb[...]
        lo[...] = xa[...]

    for r, y in enumerate(OWN_ROWS):
        used = {2: side_parts(-1)[0], N - 3: side_parts(1)[0]}.get(y, ALL)
        for i in used:
            t[r, i, pl.ds(T_AT, N)] = g_ref[r, i]
        for layer, i in x_fields(-1):
            if i in used:
                t[r, i, pl.ds(T_AT + N + layer, 1)] = hi[X_POS[-1][(layer, i)], pl.ds(y, 1)]
        for layer, i in x_fields(1):
            if i in used:
                t[r, i, pl.ds(T_AT - 1 - layer, 1)] = lo[X_POS[1][(layer, i)], pl.ds(y, 1)]

    b_out[pl.ds(Y_LEN, FAR_LEN - Y_LEN)] = jnp.zeros((FAR_LEN - Y_LEN, NZ), F32)
    for side, s in ((0, -1), (1, 1)):
        rows = [OWN_ROWS.index(y) for y in ROWS[side]]
        toward, par, away = side_parts(s)

        def moved(r, i, at=T_AT - 2, length=WIDE, steps=1):
            return zroll(t[r, i, pl.ds(at - steps * C[i][0], length)], steps * C[i][2])

        first = [moved(rows[0], i) for i in toward]
        beyond = {i: moved(rows[1], i) for i in toward}
        beside = {i: moved(rows[0], i) for i in par}
        both = {**beyond, **beside}
        mom = moments(both, toward + par)
        full = {i: moved(rows[0], i) for i in away}
        full.update({i: moved(rows[1], i) for i in par})
        full.update({i: moved(rows[2], i) for i in toward})
        relaxed = collide(full, toward)
        for k, i in enumerate(toward):
            hs[side, k, pl.ds(8, WIDE)] = relaxed[i]
        arrive = {
            i: zroll(hs[side, k, pl.ds(T_AT - C[i][0], N)], C[i][2]) for k, i in enumerate(toward)
        }
        for i in par:
            arrive[i] = KEEP * moved(rows[0], i, T_AT, N, 2)
        sums = moments(arrive, toward + par)
        parts = [(k * YW, v[:YW]) for k, v in enumerate(first)]
        parts += [((N_A + k) * YW, beyond[i][:YW]) for k, i in enumerate(toward)]
        parts += [((2 * N_A + k) * YW, v[:YW]) for k, v in enumerate((mom[0], mom[1], mom[3]))]
        parts += [(S_OFF + k * N, v) for k, v in enumerate(sums)]

        def put(out, parts=parts):
            for at, value in parts:
                out[pl.ds(at, value.shape[0])] = value

        to_a = even_y if side == 1 else jnp.logical_not(even_y)
        pl.when(to_a)(lambda put=put: put(a_out))
        pl.when(jnp.logical_not(to_a))(lambda put=put: put(b_out))


def seed_parts(seeds):
    zs = lax.rem(seeds, NZ)
    ys = lax.rem(lax.div(seeds, NZ), N)
    xs = lax.div(seeds, NZ * N)
    return xs, ys, zs


def one_hots(rx, ry, xs, ys):
    along_x = jnp.where(
        ry == ys, jnp.where(rx == xs + 1, 1.0, 0.0) - jnp.where(rx == xs - 1, 1.0, 0.0), 0.0
    )
    along_y = jnp.where(
        rx == xs, jnp.where(ry == ys + 1, 1.0, 0.0) - jnp.where(ry == ys - 1, 1.0, 0.0), 0.0
    )
    here = jnp.where((rx == xs) & (ry == ys), 1.0, 0.0)
    return jnp.concatenate([along_x, along_y, here], axis=1).astype(BF16)


def split3(v):
    hi = v.astype(BF16)
    rest = v - hi.astype(F32)
    mid = rest.astype(BF16)
    low = (rest - mid.astype(F32)).astype(BF16)
    return hi, mid, low


def picks(v, hots, zs):
    iz = lax.broadcasted_iota(jnp.int32, (NZ, SEEDS), 0)
    here = jnp.where(iz == zs, 1.0, 0.0)
    up = jnp.where(iz == lax.rem(zs + 1, NZ), 1.0, 0.0)
    down = jnp.where(iz == lax.rem(zs + NZ - 1, NZ), 1.0, 0.0)
    across = up - down
    total = None
    for part in split3(jnp.concatenate(v, axis=1)):
        got = lax.dot_general(part, hots, (((0,), (0,)), ((), ())), preferred_element_type=F32)
        total = got if total is None else total + got
    out = []
    for comp in range(3):
        for kind in range(3):
            mask = across if kind == 2 else here
            piece = total[comp * NZ : (comp + 1) * NZ, kind * SEEDS : (kind + 1) * SEEDS]
            out.append(jnp.sum(piece * mask, axis=0, keepdims=True))
    return out


def inside_kernel(f_ref, t, xa, xb, hots, seed_ref, f_out, fw_out, qw_out, pm_out, pick_out, g, h, m, v):
    even_x = lax.rem(lax.axis_index("gx"), 2) == 0

    def halo(x_hi, x_lo):
        for layer, i in x_fields(-1):
            g[i, 3 + N + layer] = x_hi[X_POS[-1][(layer, i)]]
        for layer, i in x_fields(1):
            g[i, 2 - layer] = x_lo[X_POS[1][(layer, i)]]

    pl.when(even_x)(lambda: halo(xa, xb))
    pl.when(jnp.logical_not(even_x))(lambda: halo(xb, xa))

    for side, s in ((0, 1), (1, -1)):
        rows = [OWN_ROWS.index(y) for y in ROWS[side]]
        toward, par, away = side_parts(s)
        k = 0
        for r, group in ((rows[0], par), (rows[1], away)):
            for i in group:
                fw_out[side, k] = zroll(t[r, i, pl.ds(T_AT - 2 - C[i][0], WIDE)], C[i][2])
                k += 1
        leave = {
            i: zroll(t[rows[0], i, pl.ds(T_AT - 2 - C[i][0], WIDE)], C[i][2]) for i in away
        }
        for k, value in enumerate(moments(leave, away)):
            qw_out[side, k] = value

    def first(x, _):
        out = collide([f_ref[i, pl.ds(pl.multiple_of(x * N, N), N)] for i in ALL])
        for i in ALL:
            g[i, x + 3] = out[i]
        return 0

    lax.fori_loop(0, N, first, 0, unroll=UNROLL)
    inner = lax.broadcasted_iota(jnp.int32, (N, NZ), 0)
    inner = (inner >= 1) & (inner <= N - 2)

    def shift(value, i):
        if C[i][1]:
            value = pltpu.roll(value, C[i][1] % N, axis=0)
        return zroll(value, C[i][2])

    def second(x, _):
        f = [shift(g[i, x + 1 - C[i][0]], i) for i in ALL]
        out = collide(f)
        for i in ALL:
            h[i, x] = jnp.where(inner, out[i], 0.0)
        return 0

    lax.fori_loop(0, N + 4, second, 0, unroll=UNROLL)
    iy = lax.broadcasted_iota(jnp.int32, (N, NZ), 0)
    whole = (iy >= 2) & (iy <= N - 3)

    def third(x, _):
        got = [shift(h[i, x + 1 - C[i][0]], i) for i in ALL]

        @pl.when((x >= 1) & (x <= N))
        def _():
            for i in ALL:
                f_out[i, x - 1] = got[i]

        mom = moments(got)
        for k in range(4):
            m[k, pl.ds(x * N, N)] = mom[k]
        for k in range(3):
            v[k, pl.ds(x * N, N)] = jnp.where(whole, mom[k + 1] / mom[0], 0.0)
        return 0

    lax.fori_loop(0, N + 2, third, 0, unroll=UNROLL)
    pm_out[...] = jnp.ones_like(pm_out)
    for r, y in enumerate((0, 1, 14, 15)):
        for k in range(4):
            pm_out[r, k, pl.ds(1, N + 2)] = m[k, pl.ds(y, N + 2, stride=N), :]

    zs = lax.rem(seed_ref[...], NZ)
    got = picks([v[k] for k in range(3)], hots[...], zs)
    for k in range(9):
        pick_out[pl.ds(k, 1)] = got[k]


def side_cells(side, msg, fw, qw, pm, hs, hp, ep, store):
    row_x = lax.broadcasted_iota(jnp.int32, (WIDE, NZ), 0) - 2
    near = (row_x >= -1) & (row_x <= N)
    own = (row_x >= 0) & (row_x < N)
    s = -1 if side else 1
    toward, par, away = side_parts(s)
    end, before = (N - 1, N - 2) if side else (0, 1)

    def field(k):
        return msg[pl.ds(k * YW, WIDE)]

    f = {i: field(k) for k, i in enumerate(toward)}
    f.update({i: fw[side, k] for k, i in enumerate(par + away)})
    out = collide(f)
    for i in ALL:
        hs[i, pl.ds(8, WIDE)] = out[i]
    coming = {i: field(N_A + k) for k, i in enumerate(toward)}
    mom = [
        field(2 * N_A) + qw[side, 0],
        field(2 * N_A + 1) + qw[side, 1],
        moment(coming, 1, toward) + qw[side, 2],
        field(2 * N_A + 2) + qw[side, 3],
    ]
    eq = equil(mom, toward + par)
    for k, i in enumerate(toward):
        hp[k, pl.ds(8, WIDE)] = KEEP * coming[i] + eq[i]
    for k, i in enumerate(par):
        ep[k, pl.ds(8, WIDE)] = eq[i]

    def moved(ref, k, i):
        return zroll(ref[k, pl.ds(8 - C[i][0], WIDE)], C[i][2])

    last = {i: moved(hp, k, i) for k, i in enumerate(toward)}
    last.update({i: moved(hs, i, i) for i in par})
    second = {i: moved(hs, i, i) for i in toward}
    store({i: [(end, last[i])] + ([(before, second[i])] if i in toward else []) for i in toward + par})
    vel = {}
    beyond = {i: moved(hs, i, i) for i in away}
    beyond.update({i: moved(ep, k, i) for k, i in enumerate(par)})
    for y, base, terms, group, ok in (
        (end, [pm[(3 if side else 0), k] for k in range(4)], last, toward + par, near),
        (before, [pm[(2 if side else 1), k] for k in range(4)], second, toward, near),
        (end - s, [msg[pl.ds(S_OFF + N * k - 2, WIDE)] for k in range(4)], beyond, away + par, own),
    ):
        total = [a + b for a, b in zip(base, moments(terms, group))]
        inv = 1.0 / total[0]
        vel[y] = [jnp.where(ok, total[k + 1] * inv, 0.0) for k in range(3)]
    return vel


def half_out(i, side, f_in, fs, out_hbm, sems, patches):
    for x in range(N):
        fs[i, pl.ds(x * 8, 8)] = f_in[i, x, side]
    for y, value in patches:
        fs[i, pl.ds(y - 8 * side, N, stride=8), :] = value[2 : 2 + N]
    copy = pltpu.make_async_copy(fs.at[i].reshape(N, 8, NZ), out_hbm.at[i, :, side], sems.at[i])
    copy.start()
    return copy


def side_picks(side, vel, hot, zs):
    rows = V_ROWS[3:] if side else V_ROWS[:3]
    v = [jnp.concatenate([vel[y][k] for y in rows], axis=0) for k in range(3)]
    return picks(v, hot[pl.ds(3 * WIDE * side, 3 * WIDE)], zs)


def first_side_kernel(ya, f_in, fw, qw, pm, pick, hot, seed_ref, out_hbm, pick_out, msg, hs, hp, ep, fs, sems):
    msg[pl.ds(0, Y_LEN)] = ya[...]

    def work(side):
        other = 1 - side
        copies = [pltpu.make_async_copy(f_in.at[:, :, other], out_hbm.at[:, :, other], sems.at[19])]
        copies[0].start()

        def store(patches):
            for i in ALL:
                copies.append(half_out(i, side, f_in, fs, out_hbm, sems, patches.get(i, [])))

        vel = side_cells(side, msg, fw, qw, pm, hs, hp, ep, store)
        zs = lax.rem(seed_ref[...], NZ)
        got = side_picks(side, vel, hot, zs)
        for k in range(9):
            pick_out[pl.ds(k, 1)] = got[k] + pick[pl.ds(k, 1)]
        for copy in copies:
            copy.wait()

    even = lax.rem(lax.axis_index("gy"), 2) == 0
    pl.when(even)(lambda: work(1))
    pl.when(jnp.logical_not(even))(lambda: work(0))


def second_side_kernel(
    yb, fw, qw, pm, pick, hot, seed_ref, _, out_hbm, grad_out, q_out, r_out, s_out, msg, hs, hp, ep, rows, sems
):
    msg[pl.ds(0, FAR_LEN)] = yb[...]

    def work(side):
        copies = []

        def store(patches):
            for i, changed in patches.items():
                for y, value in changed:
                    k = len(copies)
                    rows[k] = value[2 : 2 + N]
                    copies.append(pltpu.make_async_copy(rows.at[k], out_hbm.at[i, :, y], sems.at[k]))
                    copies[k].start()

        vel = side_cells(side, msg, fw, qw, pm, hs, hp, ep, store)
        zs = lax.rem(seed_ref[...], NZ)
        got = side_picks(side, vel, hot, zs)
        comps = [(got[k] + pick[pl.ds(k, 1)]) * SCALE for k in range(9)]
        q_sum = add_up(comps[3 * a + b] * comps[3 * b + a] for a in range(3) for b in range(3))
        r_sum = add_up(
            comps[3 * a + b] * comps[3 * b + c] * comps[3 * c + a]
            for a in range(3)
            for b in range(3)
            for c in range(3)
        )
        norm = add_up(c * c for c in comps)
        q = -0.5 * q_sum
        for k in range(9):
            grad_out[k, 0] = comps[k]
        q_out[0] = q
        r_out[0] = -(1.0 / 3.0) * r_sum
        s_out[0] = 2.0 * q / (norm + 0.25)
        for copy in copies:
            copy.wait()

    even = lax.rem(lax.axis_index("gy"), 2) == 0
    pl.when(even)(lambda: work(0))
    pl.when(jnp.logical_not(even))(lambda: work(1))


def swaps(count):
    first = [(i, i ^ 1) for i in range(count)]
    second = []
    for i in range(1, count, 2):
        j = (i + 1) % count
        second += [(i, j), (j, i)]
    return first, second


def shape(*dims):
    return jax.ShapeDtypeStruct(dims, F32)


VM = pl.BlockSpec(memory_space=pltpu.VMEM)
ANY = pl.BlockSpec(memory_space=pl.ANY)


def params():
    return pltpu.CompilerParams(vmem_limit_bytes=VMEM_LIMIT)


def cost(flops, moved):
    return pl.CostEstimate(flops=flops, bytes_accessed=moved, transcendentals=0)


def per_device(populations, seed_cells):
    dma = pltpu.SemaphoreType.DMA
    vmem = pltpu.VMEM
    x_first, x_second = swaps(lax.axis_size("gx"))
    y_first, y_second = swaps(lax.axis_size("gy"))
    flat = populations.reshape(19, N * N, NZ)
    seeds = seed_cells.reshape(1, SEEDS)

    xa, xb = pl.pallas_call(
        x_pack_kernel,
        out_shape=[shape(X_LEN, N, NZ)] * 2,
        in_specs=[ANY],
        out_specs=[VM] * 2,
        scratch_shapes=[vmem((2, 19, 3, N, NZ), F32), dma((2,))],
        compiler_params=params(),
        cost_estimate=cost(5_000_000, 1_500_000),
        name="x_pack",
    )(populations)
    xb = lax.ppermute(xb, "gx", x_second)
    xa = lax.ppermute(xa, "gx", x_first)
    g_rows, hot_in, hot = pl.pallas_call(
        rows_kernel,
        out_shape=[
            shape(6, 19, N, NZ),
            jax.ShapeDtypeStruct(((N + 2) * N, 3 * SEEDS), BF16),
            jax.ShapeDtypeStruct((6 * WIDE, 3 * SEEDS), BF16),
        ],
        in_specs=[VM] * 2,
        out_specs=[VM] * 3,
        compiler_params=params(),
        cost_estimate=cost(5_000_000, 3_500_000),
        name="end_rows",
    )(flat, seeds)
    ya, yb, t = pl.pallas_call(
        y_pack_kernel,
        out_shape=[shape(Y_LEN, NZ), shape(FAR_LEN, NZ), shape(6, 19, T_LEN, NZ)],
        in_specs=[VM] * 3,
        out_specs=[VM] * 3,
        scratch_shapes=[
            vmem((X_LEN, N, NZ), F32),
            vmem((X_LEN, N, NZ), F32),
            vmem((2, N_A, T_LEN, NZ), F32),
        ],
        compiler_params=params(),
        cost_estimate=cost(5_000_000, 2_000_000),
        name="y_pack",
    )(g_rows, xb, xa)
    yb = lax.ppermute(yb, "gy", y_second)
    ya = lax.ppermute(ya, "gy", y_first)
    inside, fw, qw, pm, pick = pl.pallas_call(
        inside_kernel,
        out_shape=[
            shape(19, N, N, NZ),
            shape(2, 14, WIDE, NZ),
            shape(2, 4, WIDE, NZ),
            shape(4, 4, WIDE, NZ),
            shape(9, SEEDS),
        ],
        in_specs=[VM] * 6,
        out_specs=[VM] * 5,
        scratch_shapes=[
            vmem((19, N + 6, N, NZ), F32),
            vmem((19, N + 4, N, NZ), F32),
            vmem((4, (N + 2) * N, NZ), F32),
            vmem((3, (N + 2) * N, NZ), F32),
        ],
        compiler_params=params(),
        cost_estimate=cost(50_000_000, 30_000_000),
        name="inside",
    )(flat, t, xa, xb, hot_in, seeds)
    inside = inside.reshape(19, N, 2, 8, NZ)
    side_scratch = [
        vmem((PAD_LEN, NZ), F32),
        vmem((19, T_LEN, NZ), F32),
        vmem((N_A, T_LEN, NZ), F32),
        vmem((9, T_LEN, NZ), F32),
    ]
    half, pick = pl.pallas_call(
        first_side_kernel,
        out_shape=[shape(19, N, 2, 8, NZ), shape(9, SEEDS)],
        in_specs=[VM] * 8,
        out_specs=[ANY, VM],
        scratch_shapes=side_scratch + [vmem((19, N * 8, NZ), F32), dma((20,))],
        compiler_params=params(),
        cost_estimate=cost(5_000_000, 4_000_000),
        name="first_side",
    )(ya, inside, fw, qw, pm, pick, hot, seeds)
    out, grad, q_value, r_value, share = pl.pallas_call(
        second_side_kernel,
        out_shape=[shape(19, N, N, NZ), shape(9, 1, 1, SEEDS)] + [shape(1, 1, SEEDS)] * 3,
        in_specs=[VM] * 7 + [ANY],
        out_specs=[ANY] + [VM] * 4,
        scratch_shapes=side_scratch + [vmem((19, N, NZ), F32), dma((19,))],
        input_output_aliases={7: 0},
        compiler_params=params(),
        cost_estimate=cost(5_000_000, 3_000_000),
        name="second_side",
    )(yb, fw, qw, pm, pick, hot, seeds, half.reshape(19, N, N, NZ))
    return out, grad, q_value, r_value, share


def solution(mesh):
    in_specs = (P(None, "gx", "gy", None), P("gx", "gy", None))
    out_specs = (
        P(None, "gx", "gy", None),
        P(None, "gx", "gy", None),
        P("gx", "gy", None),
        P("gx", "gy", None),
        P("gx", "gy", None),
    )
    return jax.shard_map(
        per_device, mesh=mesh, in_specs=in_specs, out_specs=out_specs, check_vma=False
    )
```

```python
import jax
import jax.numpy as jnp
from jax import lax
from jax.experimental import pallas as pl
from jax.experimental.pallas import tpu as pltpu
from jax.sharding import PartitionSpec as P

C = [
    (0, 0, 0),
    (1, 0, 0),
    (-1, 0, 0),
    (0, 1, 0),
    (0, -1, 0),
    (0, 0, 1),
    (0, 0, -1),
    (1, 1, 0),
    (-1, -1, 0),
    (1, -1, 0),
    (-1, 1, 0),
    (1, 0, 1),
    (-1, 0, -1),
    (1, 0, -1),
    (-1, 0, 1),
    (0, 1, 1),
    (0, -1, -1),
    (0, 1, -1),
    (0, -1, 1),
]
W = [1.0 / 3.0] + [1.0 / 18.0] * 6 + [1.0 / 36.0] * 12
RATE = 1.6
KEEP = 1.0 - RATE
SCALE = 10.0
ALL = list(range(19))
PAIRS = [(1, 2), (3, 4), (5, 6), (7, 8), (9, 10), (11, 12), (13, 14), (15, 16), (17, 18)]
N = 16
NZ = 128
SEEDS = 128
F32 = jnp.float32
BF16 = jnp.bfloat16
ROWS = {0: (0, 1, 2), 1: (15, 14, 13)}
OWN_ROWS = (0, 1, 2, 13, 14, 15)
T_AT = 10
T_LEN = 40
WIDE = 24
YW = 20
N_A = 5
S_OFF = 13 * YW
Y_LEN = S_OFF + 4 * N
PAD_LEN = 336
FAR_LEN = 328
V_ROWS = (-1, 0, 1, 14, 15, 16)
UNROLL = 4
VMEM_LIMIT = 28 * 1024 * 1024


def x_fields(direction):
    out = [(0, i) for i in ALL]
    out += [(1, i) for i in ALL if C[i][0] != -direction]
    out += [(2, i) for i in ALL if C[i][0] == direction]
    return out


X_POS = {d: {key: k for k, key in enumerate(x_fields(d))} for d in (-1, 1)}
X_LEN = len(X_POS[1])


def zroll(v, shift):
    shift = shift % NZ
    return pltpu.roll(v, shift, axis=v.ndim - 1) if shift else v


def add_up(terms):
    terms = list(terms)
    while len(terms) > 1:
        terms = [a + b for a, b in zip(terms[::2], terms[1::2])] + (
            [terms[-1]] if len(terms) % 2 else []
        )
    return terms[0]


def moment(f, axis, indices=ALL):
    plus = [f[i] for i in indices if C[i][axis] == 1]
    minus = [f[i] for i in indices if C[i][axis] == -1]
    if plus and minus:
        return add_up(plus) - add_up(minus)
    if plus:
        return add_up(plus)
    return -add_up(minus)


def moments(f, indices=ALL):
    return [add_up(f[i] for i in indices)] + [moment(f, axis, indices) for axis in range(3)]


def equil(mom, wanted):
    rho = mom[0]
    inv = 1.0 / rho
    u = [m * inv for m in mom[1:]]
    base = 1.0 - 1.5 * (u[0] * u[0] + u[1] * u[1] + u[2] * u[2])
    r18 = rho * (RATE / 18.0)
    r36 = rho * (RATE / 36.0)
    out = {}
    if 0 in wanted:
        out[0] = rho * (RATE / 3.0) * base
    for a, b in PAIRS:
        if a not in wanted and b not in wanted:
            continue
        along = None
        for axis in range(3):
            c = C[a][axis]
            if c:
                term = u[axis] if c == 1 else -u[axis]
                along = term if along is None else along + term
        r = r18 if a < 7 else r36
        even = r * (base + 4.5 * along * along)
        odd = r * (3.0 * along)
        if a in wanted:
            out[a] = even + odd
        if b in wanted:
            out[b] = even - odd
    return out


def collide(f, wanted=ALL):
    eq = equil(moments(f), wanted)
    return {i: KEEP * f[i] + eq[i] for i in wanted}


def side_parts(s):
    toward = [i for i in ALL if C[i][1] == s]
    par = [i for i in ALL if C[i][1] == 0]
    away = [i for i in ALL if C[i][1] == -s]
    return toward, par, away


def x_pack_kernel(low, high, a_out, b_out):
    even = lax.rem(lax.axis_index("gx"), 2) == 0
    for side, direction in ((0, -1), (1, 1)):
        buf = high if side else low
        for layer in range(3):
            at = layer if side == 0 else 2 - layer
            wanted = [i for i in ALL if (layer, i) in X_POS[direction]]
            g = collide([buf[i, at] for i in ALL], wanted)

            def put(out, layer=layer, g=g, direction=direction):
                for i, value in g.items():
                    out[X_POS[direction][(layer, i)]] = value

            first = even if side == 1 else jnp.logical_not(even)
            pl.when(first)(lambda put=put: put(a_out))
            pl.when(jnp.logical_not(first))(lambda put=put: put(b_out))


def rows_kernel(f_ref, seed_ref, g_out, inner_out, outer_out):
    for r, y in enumerate(OWN_ROWS):
        used = {2: side_parts(-1)[0], N - 3: side_parts(1)[0]}.get(y, ALL)
        g = collide([f_ref[i, pl.ds(y, N, stride=N), :] for i in ALL], used)
        for i in used:
            g_out[r, i] = g[i]
    xs, ys, _ = seed_parts(seed_ref[...])
    row = lax.broadcasted_iota(jnp.int32, ((N + 2) * N, 1), 0)
    inner_out[...] = one_hots(lax.div(row, N) - 1, lax.rem(row, N), xs, ys)
    row = lax.broadcasted_iota(jnp.int32, (6 * WIDE, 1), 0)
    block = lax.div(row, WIDE)
    ry = jnp.where(block < 3, block - 1, block + 11)
    outer_out[...] = one_hots(lax.rem(row, WIDE) - 2, ry, xs, ys)


def y_pack_kernel(g_ref, xb, xa, a_out, b_out, t, lo, hi, hs):
    even_x = lax.rem(lax.axis_index("gx"), 2) == 0
    even_y = lax.rem(lax.axis_index("gy"), 2) == 0

    @pl.when(even_x)
    def _():
        hi[...] = xa[...]
        lo[...] = xb[...]

    @pl.when(jnp.logical_not(even_x))
    def _():
        hi[...] = xb[...]
        lo[...] = xa[...]

    for r, y in enumerate(OWN_ROWS):
        used = {2: side_parts(-1)[0], N - 3: side_parts(1)[0]}.get(y, ALL)
        for i in used:
            t[r, i, pl.ds(T_AT, N)] = g_ref[r, i]
        for layer, i in x_fields(-1):
            if i in used:
                t[r, i, pl.ds(T_AT + N + layer, 1)] = hi[X_POS[-1][(layer, i)], pl.ds(y, 1)]
        for layer, i in x_fields(1):
            if i in used:
                t[r, i, pl.ds(T_AT - 1 - layer, 1)] = lo[X_POS[1][(layer, i)], pl.ds(y, 1)]

    b_out[pl.ds(Y_LEN, FAR_LEN - Y_LEN)] = jnp.zeros((FAR_LEN - Y_LEN, NZ), F32)
    for side, s in ((0, -1), (1, 1)):
        rows = [OWN_ROWS.index(y) for y in ROWS[side]]
        toward, par, away = side_parts(s)

        def moved(r, i, at=T_AT - 2, length=WIDE, steps=1):
            return zroll(t[r, i, pl.ds(at - steps * C[i][0], length)], steps * C[i][2])

        first = [moved(rows[0], i) for i in toward]
        beyond = {i: moved(rows[1], i) for i in toward}
        beside = {i: moved(rows[0], i) for i in par}
        both = {**beyond, **beside}
        mom = moments(both, toward + par)
        full = {i: moved(rows[0], i) for i in away}
        full.update({i: moved(rows[1], i) for i in par})
        full.update({i: moved(rows[2], i) for i in toward})
        relaxed = collide(full, toward)
        for k, i in enumerate(toward):
            hs[side, k, pl.ds(8, WIDE)] = relaxed[i]
        arrive = {
            i: zroll(hs[side, k, pl.ds(T_AT - C[i][0], N)], C[i][2]) for k, i in enumerate(toward)
        }
        for i in par:
            arrive[i] = KEEP * moved(rows[0], i, T_AT, N, 2)
        sums = moments(arrive, toward + par)
        parts = [(k * YW, v[:YW]) for k, v in enumerate(first)]
        parts += [((N_A + k) * YW, beyond[i][:YW]) for k, i in enumerate(toward)]
        parts += [((2 * N_A + k) * YW, v[:YW]) for k, v in enumerate((mom[0], mom[1], mom[3]))]
        parts += [(S_OFF + k * N, v) for k, v in enumerate(sums)]

        def put(out, parts=parts):
            for at, value in parts:
                out[pl.ds(at, value.shape[0])] = value

        to_a = even_y if side == 1 else jnp.logical_not(even_y)
        pl.when(to_a)(lambda put=put: put(a_out))
        pl.when(jnp.logical_not(to_a))(lambda put=put: put(b_out))


def seed_parts(seeds):
    zs = lax.rem(seeds, NZ)
    ys = lax.rem(lax.div(seeds, NZ), N)
    xs = lax.div(seeds, NZ * N)
    return xs, ys, zs


def one_hots(rx, ry, xs, ys):
    along_x = jnp.where(
        ry == ys, jnp.where(rx == xs + 1, 1.0, 0.0) - jnp.where(rx == xs - 1, 1.0, 0.0), 0.0
    )
    along_y = jnp.where(
        rx == xs, jnp.where(ry == ys + 1, 1.0, 0.0) - jnp.where(ry == ys - 1, 1.0, 0.0), 0.0
    )
    here = jnp.where((rx == xs) & (ry == ys), 1.0, 0.0)
    return jnp.concatenate([along_x, along_y, here], axis=1).astype(BF16)


def split3(v):
    hi = v.astype(BF16)
    rest = v - hi.astype(F32)
    mid = rest.astype(BF16)
    low = (rest - mid.astype(F32)).astype(BF16)
    return hi, mid, low


def picks(v, hots, zs):
    iz = lax.broadcasted_iota(jnp.int32, (NZ, SEEDS), 0)
    here = jnp.where(iz == zs, 1.0, 0.0)
    up = jnp.where(iz == lax.rem(zs + 1, NZ), 1.0, 0.0)
    down = jnp.where(iz == lax.rem(zs + NZ - 1, NZ), 1.0, 0.0)
    across = up - down
    total = None
    for part in split3(jnp.concatenate(v, axis=1)):
        got = lax.dot_general(part, hots, (((0,), (0,)), ((), ())), preferred_element_type=F32)
        total = got if total is None else total + got
    out = []
    for comp in range(3):
        for kind in range(3):
            mask = across if kind == 2 else here
            piece = total[comp * NZ : (comp + 1) * NZ, kind * SEEDS : (kind + 1) * SEEDS]
            out.append(jnp.sum(piece * mask, axis=0, keepdims=True))
    return out


def inside_kernel(f_ref, t, xa, xb, hots, seed_ref, f_out, fw_out, qw_out, pm_out, pick_out, g, h, m, v):
    even_x = lax.rem(lax.axis_index("gx"), 2) == 0

    def halo(x_hi, x_lo):
        for layer, i in x_fields(-1):
            g[i, 3 + N + layer] = x_hi[X_POS[-1][(layer, i)]]
        for layer, i in x_fields(1):
            g[i, 2 - layer] = x_lo[X_POS[1][(layer, i)]]

    pl.when(even_x)(lambda: halo(xa, xb))
    pl.when(jnp.logical_not(even_x))(lambda: halo(xb, xa))

    for side, s in ((0, 1), (1, -1)):
        rows = [OWN_ROWS.index(y) for y in ROWS[side]]
        toward, par, away = side_parts(s)
        k = 0
        for r, group in ((rows[0], par), (rows[1], away)):
            for i in group:
                fw_out[side, k] = zroll(t[r, i, pl.ds(T_AT - 2 - C[i][0], WIDE)], C[i][2])
                k += 1
        leave = {
            i: zroll(t[rows[0], i, pl.ds(T_AT - 2 - C[i][0], WIDE)], C[i][2]) for i in away
        }
        for k, value in enumerate(moments(leave, away)):
            qw_out[side, k] = value

    def first(x, _):
        out = collide([f_ref[i, pl.ds(pl.multiple_of(x * N, N), N)] for i in ALL])
        for i in ALL:
            g[i, x + 3] = out[i]
        return 0

    lax.fori_loop(0, N, first, 0, unroll=UNROLL)
    inner = lax.broadcasted_iota(jnp.int32, (N, NZ), 0)
    inner = (inner >= 1) & (inner <= N - 2)

    def shift(value, i):
        if C[i][1]:
            value = pltpu.roll(value, C[i][1] % N, axis=0)
        return zroll(value, C[i][2])

    def second(x, _):
        f = [shift(g[i, x + 1 - C[i][0]], i) for i in ALL]
        out = collide(f)
        for i in ALL:
            h[i, x] = jnp.where(inner, out[i], 0.0)
        return 0

    lax.fori_loop(0, N + 4, second, 0, unroll=UNROLL)
    iy = lax.broadcasted_iota(jnp.int32, (N, NZ), 0)
    whole = (iy >= 2) & (iy <= N - 3)

    def third(x, _):
        got = [shift(h[i, x + 1 - C[i][0]], i) for i in ALL]

        @pl.when((x >= 1) & (x <= N))
        def _():
            for i in ALL:
                f_out[i, x - 1] = got[i]

        mom = moments(got)
        for k in range(4):
            m[k, pl.ds(x * N, N)] = mom[k]
        for k in range(3):
            v[k, pl.ds(x * N, N)] = jnp.where(whole, mom[k + 1] / mom[0], 0.0)
        return 0

    lax.fori_loop(0, N + 2, third, 0, unroll=UNROLL)
    pm_out[...] = jnp.ones_like(pm_out)
    for r, y in enumerate((0, 1, 14, 15)):
        for k in range(4):
            pm_out[r, k, pl.ds(1, N + 2)] = m[k, pl.ds(y, N + 2, stride=N), :]

    zs = lax.rem(seed_ref[...], NZ)
    got = picks([v[k] for k in range(3)], hots[...], zs)
    for k in range(9):
        pick_out[pl.ds(k, 1)] = got[k]


def side_cells(side, msg, fw, qw, pm, hs, hp, ep, store):
    row_x = lax.broadcasted_iota(jnp.int32, (WIDE, NZ), 0) - 2
    near = (row_x >= -1) & (row_x <= N)
    own = (row_x >= 0) & (row_x < N)
    s = -1 if side else 1
    toward, par, away = side_parts(s)
    end, before = (N - 1, N - 2) if side else (0, 1)

    def field(k):
        return msg[pl.ds(k * YW, WIDE)]

    f = {i: field(k) for k, i in enumerate(toward)}
    f.update({i: fw[side, k] for k, i in enumerate(par + away)})
    out = collide(f)
    for i in ALL:
        hs[i, pl.ds(8, WIDE)] = out[i]
    coming = {i: field(N_A + k) for k, i in enumerate(toward)}
    mom = [
        field(2 * N_A) + qw[side, 0],
        field(2 * N_A + 1) + qw[side, 1],
        moment(coming, 1, toward) + qw[side, 2],
        field(2 * N_A + 2) + qw[side, 3],
    ]
    eq = equil(mom, toward + par)
    for k, i in enumerate(toward):
        hp[k, pl.ds(8, WIDE)] = KEEP * coming[i] + eq[i]
    for k, i in enumerate(par):
        ep[k, pl.ds(8, WIDE)] = eq[i]

    def moved(ref, k, i):
        return zroll(ref[k, pl.ds(8 - C[i][0], WIDE)], C[i][2])

    last = {i: moved(hp, k, i) for k, i in enumerate(toward)}
    last.update({i: moved(hs, i, i) for i in par})
    second = {i: moved(hs, i, i) for i in toward}
    store({i: [(end, last[i])] + ([(before, second[i])] if i in toward else []) for i in toward + par})
    vel = {}
    beyond = {i: moved(hs, i, i) for i in away}
    beyond.update({i: moved(ep, k, i) for k, i in enumerate(par)})
    for y, base, terms, group, ok in (
        (end, [pm[(3 if side else 0), k] for k in range(4)], last, toward + par, near),
        (before, [pm[(2 if side else 1), k] for k in range(4)], second, toward, near),
        (end - s, [msg[pl.ds(S_OFF + N * k - 2, WIDE)] for k in range(4)], beyond, away + par, own),
    ):
        total = [a + b for a, b in zip(base, moments(terms, group))]
        inv = 1.0 / total[0]
        vel[y] = [jnp.where(ok, total[k + 1] * inv, 0.0) for k in range(3)]
    return vel


def half_out(i, side, f_in, fs, out_hbm, sems, patches):
    for x in range(N):
        fs[i, pl.ds(x * 8, 8)] = f_in[i, x, side]
    for y, value in patches:
        fs[i, pl.ds(y - 8 * side, N, stride=8), :] = value[2 : 2 + N]
    copy = pltpu.make_async_copy(fs.at[i].reshape(N, 8, NZ), out_hbm.at[i, :, side], sems.at[i])
    copy.start()
    return copy


def side_picks(side, vel, hot, zs):
    rows = V_ROWS[3:] if side else V_ROWS[:3]
    v = [jnp.concatenate([vel[y][k] for y in rows], axis=0) for k in range(3)]
    return picks(v, hot[pl.ds(3 * WIDE * side, 3 * WIDE)], zs)


def first_side_kernel(ya, f_in, fw, qw, pm, pick, hot, seed_ref, out_hbm, pick_out, msg, hs, hp, ep, fs, sems):
    msg[pl.ds(0, Y_LEN)] = ya[...]

    def work(side):
        other = 1 - side
        copies = [pltpu.make_async_copy(f_in.at[:, :, other], out_hbm.at[:, :, other], sems.at[19])]
        copies[0].start()

        def store(patches):
            for i in ALL:
                copies.append(half_out(i, side, f_in, fs, out_hbm, sems, patches.get(i, [])))

        vel = side_cells(side, msg, fw, qw, pm, hs, hp, ep, store)
        zs = lax.rem(seed_ref[...], NZ)
        got = side_picks(side, vel, hot, zs)
        for k in range(9):
            pick_out[pl.ds(k, 1)] = got[k] + pick[pl.ds(k, 1)]
        for copy in copies:
            copy.wait()

    even = lax.rem(lax.axis_index("gy"), 2) == 0
    pl.when(even)(lambda: work(1))
    pl.when(jnp.logical_not(even))(lambda: work(0))


def second_side_kernel(
    yb, fw, qw, pm, pick, hot, seed_ref, _, out_hbm, grad_out, q_out, r_out, s_out, msg, hs, hp, ep, rows, sems
):
    msg[pl.ds(0, FAR_LEN)] = yb[...]

    def work(side):
        copies = []

        def store(patches):
            for i, changed in patches.items():
                for y, value in changed:
                    k = len(copies)
                    rows[k] = value[2 : 2 + N]
                    copies.append(pltpu.make_async_copy(rows.at[k], out_hbm.at[i, :, y], sems.at[k]))
                    copies[k].start()

        vel = side_cells(side, msg, fw, qw, pm, hs, hp, ep, store)
        zs = lax.rem(seed_ref[...], NZ)
        got = side_picks(side, vel, hot, zs)
        comps = [(got[k] + pick[pl.ds(k, 1)]) * SCALE for k in range(9)]
        q_sum = add_up(comps[3 * a + b] * comps[3 * b + a] for a in range(3) for b in range(3))
        r_sum = add_up(
            comps[3 * a + b] * comps[3 * b + c] * comps[3 * c + a]
            for a in range(3)
            for b in range(3)
            for c in range(3)
        )
        norm = add_up(c * c for c in comps)
        q = -0.5 * q_sum
        for k in range(9):
            grad_out[k, 0] = comps[k]
        q_out[0] = q
        r_out[0] = -(1.0 / 3.0) * r_sum
        s_out[0] = 2.0 * q / (norm + 0.25)
        for copy in copies:
            copy.wait()

    even = lax.rem(lax.axis_index("gy"), 2) == 0
    pl.when(even)(lambda: work(0))
    pl.when(jnp.logical_not(even))(lambda: work(1))


def swaps(count):
    first = [(i, i ^ 1) for i in range(count)]
    second = []
    for i in range(1, count, 2):
        j = (i + 1) % count
        second += [(i, j), (j, i)]
    return first, second


def shape(*dims):
    return jax.ShapeDtypeStruct(dims, F32)


VM = pl.BlockSpec(memory_space=pltpu.VMEM)
ANY = pl.BlockSpec(memory_space=pl.ANY)


def params():
    return pltpu.CompilerParams(vmem_limit_bytes=VMEM_LIMIT)


def cost(flops, moved):
    return pl.CostEstimate(flops=flops, bytes_accessed=moved, transcendentals=0)


def per_device(populations, seed_cells):
    dma = pltpu.SemaphoreType.DMA
    vmem = pltpu.VMEM
    x_first, x_second = swaps(lax.axis_size("gx"))
    y_first, y_second = swaps(lax.axis_size("gy"))
    flat = populations.reshape(19, N * N, NZ)
    seeds = seed_cells.reshape(1, SEEDS)

    xa, xb = pl.pallas_call(
        x_pack_kernel,
        out_shape=[shape(X_LEN, N, NZ)] * 2,
        in_specs=[VM] * 2,
        out_specs=[VM] * 2,
        compiler_params=params(),
        cost_estimate=cost(5_000_000, 1_500_000),
        name="x_pack",
    )(populations[:, :3], populations[:, N - 3 :])
    xb = lax.ppermute(xb, "gx", x_second)
    xa = lax.ppermute(xa, "gx", x_first)
    g_rows, hot_in, hot = pl.pallas_call(
        rows_kernel,
        out_shape=[
            shape(6, 19, N, NZ),
            jax.ShapeDtypeStruct(((N + 2) * N, 3 * SEEDS), BF16),
            jax.ShapeDtypeStruct((6 * WIDE, 3 * SEEDS), BF16),
        ],
        in_specs=[VM] * 2,
        out_specs=[VM] * 3,
        compiler_params=params(),
        cost_estimate=cost(5_000_000, 3_500_000),
        name="end_rows",
    )(flat, seeds)
    ya, yb, t = pl.pallas_call(
        y_pack_kernel,
        out_shape=[shape(Y_LEN, NZ), shape(FAR_LEN, NZ), shape(6, 19, T_LEN, NZ)],
        in_specs=[VM] * 3,
        out_specs=[VM] * 3,
        scratch_shapes=[
            vmem((X_LEN, N, NZ), F32),
            vmem((X_LEN, N, NZ), F32),
            vmem((2, N_A, T_LEN, NZ), F32),
        ],
        compiler_params=params(),
        cost_estimate=cost(5_000_000, 2_000_000),
        name="y_pack",
    )(g_rows, xb, xa)
    yb = lax.ppermute(yb, "gy", y_second)
    ya = lax.ppermute(ya, "gy", y_first)
    inside, fw, qw, pm, pick = pl.pallas_call(
        inside_kernel,
        out_shape=[
            shape(19, N, N, NZ),
            shape(2, 14, WIDE, NZ),
            shape(2, 4, WIDE, NZ),
            shape(4, 4, WIDE, NZ),
            shape(9, SEEDS),
        ],
        in_specs=[VM] * 6,
        out_specs=[VM] * 5,
        scratch_shapes=[
            vmem((19, N + 6, N, NZ), F32),
            vmem((19, N + 4, N, NZ), F32),
            vmem((4, (N + 2) * N, NZ), F32),
            vmem((3, (N + 2) * N, NZ), F32),
        ],
        compiler_params=params(),
        cost_estimate=cost(50_000_000, 30_000_000),
        name="inside",
    )(flat, t, xa, xb, hot_in, seeds)
    inside = inside.reshape(19, N, 2, 8, NZ)
    side_scratch = [
        vmem((PAD_LEN, NZ), F32),
        vmem((19, T_LEN, NZ), F32),
        vmem((N_A, T_LEN, NZ), F32),
        vmem((9, T_LEN, NZ), F32),
    ]
    half, pick = pl.pallas_call(
        first_side_kernel,
        out_shape=[shape(19, N, 2, 8, NZ), shape(9, SEEDS)],
        in_specs=[VM] * 8,
        out_specs=[ANY, VM],
        scratch_shapes=side_scratch + [vmem((19, N * 8, NZ), F32), dma((20,))],
        compiler_params=params(),
        cost_estimate=cost(5_000_000, 4_000_000),
        name="first_side",
    )(ya, inside, fw, qw, pm, pick, hot, seeds)
    out, grad, q_value, r_value, share = pl.pallas_call(
        second_side_kernel,
        out_shape=[shape(19, N, N, NZ), shape(9, 1, 1, SEEDS)] + [shape(1, 1, SEEDS)] * 3,
        in_specs=[VM] * 7 + [ANY],
        out_specs=[ANY] + [VM] * 4,
        scratch_shapes=side_scratch + [vmem((19, N, NZ), F32), dma((19,))],
        input_output_aliases={7: 0},
        compiler_params=params(),
        cost_estimate=cost(5_000_000, 3_000_000),
        name="second_side",
    )(yb, fw, qw, pm, pick, hot, seeds, half.reshape(19, N, N, NZ))
    return out, grad, q_value, r_value, share


def solution(mesh):
    in_specs = (P(None, "gx", "gy", None), P("gx", "gy", None))
    out_specs = (
        P(None, "gx", "gy", None),
        P(None, "gx", "gy", None),
        P("gx", "gy", None),
        P("gx", "gy", None),
        P("gx", "gy", None),
    )
    return jax.shard_map(
        per_device, mesh=mesh, in_specs=in_specs, out_specs=out_specs, check_vma=False
    )
```

```python
import jax
import jax.numpy as jnp
from jax import lax
from jax.experimental import pallas as pl
from jax.experimental.pallas import tpu as pltpu
from jax.sharding import PartitionSpec as P

C = [
    (0, 0, 0),
    (1, 0, 0),
    (-1, 0, 0),
    (0, 1, 0),
    (0, -1, 0),
    (0, 0, 1),
    (0, 0, -1),
    (1, 1, 0),
    (-1, -1, 0),
    (1, -1, 0),
    (-1, 1, 0),
    (1, 0, 1),
    (-1, 0, -1),
    (1, 0, -1),
    (-1, 0, 1),
    (0, 1, 1),
    (0, -1, -1),
    (0, 1, -1),
    (0, -1, 1),
]
W = [1.0 / 3.0] + [1.0 / 18.0] * 6 + [1.0 / 36.0] * 12
RATE = 1.6
KEEP = 1.0 - RATE
SCALE = 10.0
ALL = list(range(19))
PAIRS = [(1, 2), (3, 4), (5, 6), (7, 8), (9, 10), (11, 12), (13, 14), (15, 16), (17, 18)]
N = 16
NZ = 128
SEEDS = 128
F32 = jnp.float32
BF16 = jnp.bfloat16
ROWS = {0: (0, 1, 2), 1: (15, 14, 13)}
OWN_ROWS = (0, 1, 2, 13, 14, 15)
T_AT = 10
T_LEN = 40
WIDE = 24
YW = 20
N_A = 5
BW = 18
B_OFF = N_A * YW
P_OFF = B_OFF + N_A * BW
S_OFF = P_OFF + 3 * YW
E_OFF = S_OFF + 4 * N
Y_LEN = E_OFF + 4
PAD_LEN = 336
FAR_LEN = 320
V_ROWS = (-1, 0, 1, 14, 15, 16)
UNROLL = 4
VMEM_LIMIT = 28 * 1024 * 1024


def x_fields(direction):
    out = [(0, i) for i in ALL]
    out += [(1, i) for i in ALL if C[i][0] != -direction]
    out += [(2, i) for i in ALL if C[i][0] == direction]
    return out


X_POS = {d: {key: k for k, key in enumerate(x_fields(d))} for d in (-1, 1)}
X_LEN = len(X_POS[1])


def zroll(v, shift):
    shift = shift % NZ
    return pltpu.roll(v, shift, axis=v.ndim - 1) if shift else v


def add_up(terms):
    terms = list(terms)
    while len(terms) > 1:
        terms = [a + b for a, b in zip(terms[::2], terms[1::2])] + (
            [terms[-1]] if len(terms) % 2 else []
        )
    return terms[0]


def moment(f, axis, indices=ALL):
    plus = [f[i] for i in indices if C[i][axis] == 1]
    minus = [f[i] for i in indices if C[i][axis] == -1]
    if plus and minus:
        return add_up(plus) - add_up(minus)
    if plus:
        return add_up(plus)
    return -add_up(minus)


def moments(f, indices=ALL):
    return [add_up(f[i] for i in indices)] + [moment(f, axis, indices) for axis in range(3)]


def equil(mom, wanted):
    rho = mom[0]
    inv = 1.0 / rho
    u = [m * inv for m in mom[1:]]
    base = 1.0 - 1.5 * (u[0] * u[0] + u[1] * u[1] + u[2] * u[2])
    r18 = rho * (RATE / 18.0)
    r36 = rho * (RATE / 36.0)
    out = {}
    if 0 in wanted:
        out[0] = rho * (RATE / 3.0) * base
    for a, b in PAIRS:
        if a not in wanted and b not in wanted:
            continue
        along = None
        for axis in range(3):
            c = C[a][axis]
            if c:
                term = u[axis] if c == 1 else -u[axis]
                along = term if along is None else along + term
        r = r18 if a < 7 else r36
        even = r * (base + 4.5 * along * along)
        odd = r * (3.0 * along)
        if a in wanted:
            out[a] = even + odd
        if b in wanted:
            out[b] = even - odd
    return out


def collide(f, wanted=ALL):
    eq = equil(moments(f), wanted)
    return {i: KEEP * f[i] + eq[i] for i in wanted}


def side_parts(s):
    toward = [i for i in ALL if C[i][1] == s]
    par = [i for i in ALL if C[i][1] == 0]
    away = [i for i in ALL if C[i][1] == -s]
    return toward, par, away


def x_pack_kernel(low, high, a_out, b_out):
    even = lax.rem(lax.axis_index("gx"), 2) == 0
    for side, direction in ((0, -1), (1, 1)):
        buf = high if side else low
        for layer in range(3):
            at = layer if side == 0 else 2 - layer
            wanted = [i for i in ALL if (layer, i) in X_POS[direction]]
            g = collide([buf[i, at] for i in ALL], wanted)

            def put(out, layer=layer, g=g, direction=direction):
                for i, value in g.items():
                    out[X_POS[direction][(layer, i)]] = value

            first = even if side == 1 else jnp.logical_not(even)
            pl.when(first)(lambda put=put: put(a_out))
            pl.when(jnp.logical_not(first))(lambda put=put: put(b_out))


def rows_kernel(f_ref, seed_ref, g_out, inner_out, outer_out):
    for r, y in enumerate(OWN_ROWS):
        used = {2: side_parts(-1)[0], N - 3: side_parts(1)[0]}.get(y, ALL)
        g = collide([f_ref[i, pl.ds(y, N, stride=N), :] for i in ALL], used)
        for i in used:
            g_out[r, i] = g[i]
    xs, ys, _ = seed_parts(seed_ref[...])
    row = lax.broadcasted_iota(jnp.int32, ((N + 2) * N, 1), 0)
    inner_out[...] = one_hots(lax.div(row, N) - 1, lax.rem(row, N), xs, ys)
    row = lax.broadcasted_iota(jnp.int32, (6 * WIDE, 1), 0)
    block = lax.div(row, WIDE)
    ry = jnp.where(block < 3, block - 1, block + 11)
    outer_out[...] = one_hots(lax.rem(row, WIDE) - 2, ry, xs, ys)


def y_pack_kernel(g_ref, xb, xa, a_out, b_out, t, lo, hi, hs):
    even_x = lax.rem(lax.axis_index("gx"), 2) == 0
    even_y = lax.rem(lax.axis_index("gy"), 2) == 0

    @pl.when(even_x)
    def _():
        hi[...] = xa[...]
        lo[...] = xb[...]

    @pl.when(jnp.logical_not(even_x))
    def _():
        hi[...] = xb[...]
        lo[...] = xa[...]

    for r, y in enumerate(OWN_ROWS):
        used = {2: side_parts(-1)[0], N - 3: side_parts(1)[0]}.get(y, ALL)
        for i in used:
            t[r, i, pl.ds(T_AT, N)] = g_ref[r, i]
        for layer, i in x_fields(-1):
            if i in used:
                t[r, i, pl.ds(T_AT + N + layer, 1)] = hi[X_POS[-1][(layer, i)], pl.ds(y, 1)]
        for layer, i in x_fields(1):
            if i in used:
                t[r, i, pl.ds(T_AT - 1 - layer, 1)] = lo[X_POS[1][(layer, i)], pl.ds(y, 1)]

    b_out[pl.ds(Y_LEN, FAR_LEN - Y_LEN)] = jnp.zeros((FAR_LEN - Y_LEN, NZ), F32)
    for side, s in ((0, -1), (1, 1)):
        rows = [OWN_ROWS.index(y) for y in ROWS[side]]
        toward, par, away = side_parts(s)

        def moved(r, i, at=T_AT - 2, length=WIDE, steps=1):
            return zroll(t[r, i, pl.ds(at - steps * C[i][0], length)], steps * C[i][2])

        first = [moved(rows[0], i) for i in toward]
        beyond = {i: moved(rows[1], i) for i in toward}
        beside = {i: moved(rows[0], i) for i in par}
        both = {**beyond, **beside}
        mom = moments(both, toward + par)
        full = {i: moved(rows[0], i) for i in away}
        full.update({i: moved(rows[1], i) for i in par})
        full.update({i: moved(rows[2], i) for i in toward})
        relaxed = collide(full, toward)
        for k, i in enumerate(toward):
            hs[side, k, pl.ds(8, WIDE)] = relaxed[i]
        arrive = {
            i: zroll(hs[side, k, pl.ds(T_AT - C[i][0], N)], C[i][2]) for k, i in enumerate(toward)
        }
        for i in par:
            arrive[i] = KEEP * moved(rows[0], i, T_AT, N, 2)
        sums = moments(arrive, toward + par)
        parts = [(k * YW, v[:YW]) for k, v in enumerate(first)]
        parts += [(B_OFF + k * BW, beyond[i][1 : 1 + BW]) for k, i in enumerate(toward)]
        parts += [(P_OFF + k * YW, v[:YW]) for k, v in enumerate((mom[0], mom[1], mom[3]))]
        for k, (at, inward) in enumerate(((0, 1), (YW - 1, -1))):
            alone = [i for i in toward if C[i][0] == inward][0]
            others = add_up(beyond[i] for i in toward if i != alone)
            parts += [(E_OFF + 2 * k, beyond[alone][at : at + 1]), (E_OFF + 2 * k + 1, others[at : at + 1])]
        parts += [(S_OFF + k * N, v) for k, v in enumerate(sums)]

        def put(out, parts=parts):
            for at, value in parts:
                out[pl.ds(at, value.shape[0])] = value

        to_a = even_y if side == 1 else jnp.logical_not(even_y)
        pl.when(to_a)(lambda put=put: put(a_out))
        pl.when(jnp.logical_not(to_a))(lambda put=put: put(b_out))


def seed_parts(seeds):
    zs = lax.rem(seeds, NZ)
    ys = lax.rem(lax.div(seeds, NZ), N)
    xs = lax.div(seeds, NZ * N)
    return xs, ys, zs


def one_hots(rx, ry, xs, ys):
    along_x = jnp.where(
        ry == ys, jnp.where(rx == xs + 1, 1.0, 0.0) - jnp.where(rx == xs - 1, 1.0, 0.0), 0.0
    )
    along_y = jnp.where(
        rx == xs, jnp.where(ry == ys + 1, 1.0, 0.0) - jnp.where(ry == ys - 1, 1.0, 0.0), 0.0
    )
    here = jnp.where((rx == xs) & (ry == ys), 1.0, 0.0)
    return jnp.concatenate([along_x, along_y, here], axis=1).astype(BF16)


def split3(v):
    hi = v.astype(BF16)
    rest = v - hi.astype(F32)
    mid = rest.astype(BF16)
    low = (rest - mid.astype(F32)).astype(BF16)
    return hi, mid, low


def picks(v, hots, zs):
    iz = lax.broadcasted_iota(jnp.int32, (NZ, SEEDS), 0)
    here = jnp.where(iz == zs, 1.0, 0.0)
    up = jnp.where(iz == lax.rem(zs + 1, NZ), 1.0, 0.0)
    down = jnp.where(iz == lax.rem(zs + NZ - 1, NZ), 1.0, 0.0)
    across = up - down
    total = None
    for part in split3(jnp.concatenate(v, axis=1)):
        got = lax.dot_general(part, hots, (((0,), (0,)), ((), ())), preferred_element_type=F32)
        total = got if total is None else total + got
    out = []
    for comp in range(3):
        for kind in range(3):
            mask = across if kind == 2 else here
            piece = total[comp * NZ : (comp + 1) * NZ, kind * SEEDS : (kind + 1) * SEEDS]
            out.append(jnp.sum(piece * mask, axis=0, keepdims=True))
    return out


def inside_kernel(f_ref, t, xa, xb, hots, seed_ref, f_out, fw_out, qw_out, pm_out, pick_out, g, h, m, v):
    even_x = lax.rem(lax.axis_index("gx"), 2) == 0

    def halo(x_hi, x_lo):
        for layer, i in x_fields(-1):
            g[i, 3 + N + layer] = x_hi[X_POS[-1][(layer, i)]]
        for layer, i in x_fields(1):
            g[i, 2 - layer] = x_lo[X_POS[1][(layer, i)]]

    pl.when(even_x)(lambda: halo(xa, xb))
    pl.when(jnp.logical_not(even_x))(lambda: halo(xb, xa))

    for side, s in ((0, 1), (1, -1)):
        rows = [OWN_ROWS.index(y) for y in ROWS[side]]
        toward, par, away = side_parts(s)
        k = 0
        for r, group in ((rows[0], par), (rows[1], away)):
            for i in group:
                fw_out[side, k] = zroll(t[r, i, pl.ds(T_AT - 2 - C[i][0], WIDE)], C[i][2])
                k += 1
        leave = {
            i: zroll(t[rows[0], i, pl.ds(T_AT - 2 - C[i][0], WIDE)], C[i][2]) for i in away
        }
        for k, value in enumerate(moments(leave, away)):
            qw_out[side, k] = value

    def first(x, _):
        out = collide([f_ref[i, pl.ds(pl.multiple_of(x * N, N), N)] for i in ALL])
        for i in ALL:
            g[i, x + 3] = out[i]
        return 0

    lax.fori_loop(0, N, first, 0, unroll=UNROLL)
    inner = lax.broadcasted_iota(jnp.int32, (N, NZ), 0)
    inner = (inner >= 1) & (inner <= N - 2)

    def shift(value, i):
        if C[i][1]:
            value = pltpu.roll(value, C[i][1] % N, axis=0)
        return zroll(value, C[i][2])

    def second(x, _):
        f = [shift(g[i, x + 1 - C[i][0]], i) for i in ALL]
        out = collide(f)
        for i in ALL:
            h[i, x] = jnp.where(inner, out[i], 0.0)
        return 0

    lax.fori_loop(0, N + 4, second, 0, unroll=UNROLL)
    iy = lax.broadcasted_iota(jnp.int32, (N, NZ), 0)
    whole = (iy >= 2) & (iy <= N - 3)

    def third(x, _):
        got = [shift(h[i, x + 1 - C[i][0]], i) for i in ALL]

        @pl.when((x >= 1) & (x <= N))
        def _():
            for i in ALL:
                f_out[i, x - 1] = got[i]

        mom = moments(got)
        for k in range(4):
            m[k, pl.ds(x * N, N)] = mom[k]
        for k in range(3):
            v[k, pl.ds(x * N, N)] = jnp.where(whole, mom[k + 1] / mom[0], 0.0)
        return 0

    lax.fori_loop(0, N + 2, third, 0, unroll=UNROLL)
    pm_out[...] = jnp.ones_like(pm_out)
    for r, y in enumerate((0, 1, 14, 15)):
        for k in range(4):
            pm_out[r, k, pl.ds(1, N + 2)] = m[k, pl.ds(y, N + 2, stride=N), :]

    zs = lax.rem(seed_ref[...], NZ)
    got = picks([v[k] for k in range(3)], hots[...], zs)
    for k in range(9):
        pick_out[pl.ds(k, 1)] = got[k]


def side_cells(side, msg, fw, qw, pm, hs, hp, ep, cb, store):
    row_x = lax.broadcasted_iota(jnp.int32, (WIDE, NZ), 0) - 2
    near = (row_x >= -1) & (row_x <= N)
    own = (row_x >= 0) & (row_x < N)
    s = -1 if side else 1
    toward, par, away = side_parts(s)
    end, before = (N - 1, N - 2) if side else (0, 1)

    def field(k):
        return msg[pl.ds(k * YW, WIDE)]

    f = {i: field(k) for k, i in enumerate(toward)}
    f.update({i: fw[side, k] for k, i in enumerate(par + away)})
    out = collide(f)
    for i in ALL:
        hs[i, pl.ds(8, WIDE)] = out[i]
    cb[...] = jnp.zeros_like(cb)
    for k in range(N_A):
        cb[k, pl.ds(1, BW)] = msg[pl.ds(B_OFF + k * BW, BW)]
    middle = [k for k, i in enumerate(toward) if C[i][0] == 0][0]
    for k, (at, inward) in enumerate(((0, 1), (YW - 1, -1))):
        alone = [k for k, i in enumerate(toward) if C[i][0] == inward][0]
        cb[alone, pl.ds(at, 1)] = msg[pl.ds(E_OFF + 2 * k, 1)]
        cb[middle, pl.ds(at, 1)] = msg[pl.ds(E_OFF + 2 * k + 1, 1)]
    coming = {i: cb[k] for k, i in enumerate(toward)}
    part = [msg[pl.ds(P_OFF + k * YW, WIDE)] for k in range(3)]
    mom = [
        part[0] + qw[side, 0],
        part[1] + qw[side, 1],
        moment(coming, 1, toward) + qw[side, 2],
        part[2] + qw[side, 3],
    ]
    eq = equil(mom, toward + par)
    for k, i in enumerate(toward):
        hp[k, pl.ds(8, WIDE)] = KEEP * coming[i] + eq[i]
    for k, i in enumerate(par):
        ep[k, pl.ds(8, WIDE)] = eq[i]

    def moved(ref, k, i):
        return zroll(ref[k, pl.ds(8 - C[i][0], WIDE)], C[i][2])

    last = {i: moved(hp, k, i) for k, i in enumerate(toward)}
    last.update({i: moved(hs, i, i) for i in par})
    second = {i: moved(hs, i, i) for i in toward}
    store({i: [(end, last[i])] + ([(before, second[i])] if i in toward else []) for i in toward + par})
    vel = {}
    beyond = {i: moved(hs, i, i) for i in away}
    beyond.update({i: moved(ep, k, i) for k, i in enumerate(par)})
    for y, base, terms, group, ok in (
        (end, [pm[(3 if side else 0), k] for k in range(4)], last, toward + par, near),
        (before, [pm[(2 if side else 1), k] for k in range(4)], second, toward, near),
        (end - s, [msg[pl.ds(S_OFF + N * k - 2, WIDE)] for k in range(4)], beyond, away + par, own),
    ):
        total = [a + b for a, b in zip(base, moments(terms, group))]
        inv = 1.0 / total[0]
        vel[y] = [jnp.where(ok, total[k + 1] * inv, 0.0) for k in range(3)]
    return vel


def half_out(i, side, f_in, fs, out_hbm, sems, patches):
    for x in range(N):
        fs[i, pl.ds(x * 8, 8)] = f_in[i, x, side]
    for y, value in patches:
        fs[i, pl.ds(y - 8 * side, N, stride=8), :] = value[2 : 2 + N]
    copy = pltpu.make_async_copy(fs.at[i].reshape(N, 8, NZ), out_hbm.at[i, :, side], sems.at[i])
    copy.start()
    return copy


def side_picks(side, vel, hot, zs):
    rows = V_ROWS[3:] if side else V_ROWS[:3]
    v = [jnp.concatenate([vel[y][k] for y in rows], axis=0) for k in range(3)]
    return picks(v, hot[pl.ds(3 * WIDE * side, 3 * WIDE)], zs)


def first_side_kernel(ya, f_in, fw, qw, pm, pick, hot, seed_ref, out_hbm, pick_out, msg, hs, hp, ep, cb, fs, sems):
    msg[pl.ds(0, Y_LEN)] = ya[...]

    def work(side):
        other = 1 - side
        copies = [pltpu.make_async_copy(f_in.at[:, :, other], out_hbm.at[:, :, other], sems.at[19])]
        copies[0].start()

        def store(patches):
            for i in ALL:
                copies.append(half_out(i, side, f_in, fs, out_hbm, sems, patches.get(i, [])))

        vel = side_cells(side, msg, fw, qw, pm, hs, hp, ep, cb, store)
        zs = lax.rem(seed_ref[...], NZ)
        got = side_picks(side, vel, hot, zs)
        for k in range(9):
            pick_out[pl.ds(k, 1)] = got[k] + pick[pl.ds(k, 1)]
        for copy in copies:
            copy.wait()

    even = lax.rem(lax.axis_index("gy"), 2) == 0
    pl.when(even)(lambda: work(1))
    pl.when(jnp.logical_not(even))(lambda: work(0))


def second_side_kernel(
    yb, fw, qw, pm, pick, hot, seed_ref, _, out_hbm, grad_out, q_out, r_out, s_out, msg, hs, hp, ep, cb, rows, sems
):
    msg[pl.ds(0, FAR_LEN)] = yb[...]

    def work(side):
        copies = []

        def store(patches):
            for i, changed in patches.items():
                for y, value in changed:
                    k = len(copies)
                    rows[k] = value[2 : 2 + N]
                    copies.append(pltpu.make_async_copy(rows.at[k], out_hbm.at[i, :, y], sems.at[k]))
                    copies[k].start()

        vel = side_cells(side, msg, fw, qw, pm, hs, hp, ep, cb, store)
        zs = lax.rem(seed_ref[...], NZ)
        got = side_picks(side, vel, hot, zs)
        comps = [(got[k] + pick[pl.ds(k, 1)]) * SCALE for k in range(9)]
        q_sum = add_up(comps[3 * a + b] * comps[3 * b + a] for a in range(3) for b in range(3))
        r_sum = add_up(
            comps[3 * a + b] * comps[3 * b + c] * comps[3 * c + a]
            for a in range(3)
            for b in range(3)
            for c in range(3)
        )
        norm = add_up(c * c for c in comps)
        q = -0.5 * q_sum
        for k in range(9):
            grad_out[k, 0] = comps[k]
        q_out[0] = q
        r_out[0] = -(1.0 / 3.0) * r_sum
        s_out[0] = 2.0 * q / (norm + 0.25)
        for copy in copies:
            copy.wait()

    even = lax.rem(lax.axis_index("gy"), 2) == 0
    pl.when(even)(lambda: work(0))
    pl.when(jnp.logical_not(even))(lambda: work(1))


def swaps(count):
    first = [(i, i ^ 1) for i in range(count)]
    second = []
    for i in range(1, count, 2):
        j = (i + 1) % count
        second += [(i, j), (j, i)]
    return first, second


def shape(*dims):
    return jax.ShapeDtypeStruct(dims, F32)


VM = pl.BlockSpec(memory_space=pltpu.VMEM)
ANY = pl.BlockSpec(memory_space=pl.ANY)


def params():
    return pltpu.CompilerParams(vmem_limit_bytes=VMEM_LIMIT)


def cost(flops, moved):
    return pl.CostEstimate(flops=flops, bytes_accessed=moved, transcendentals=0)


def per_device(populations, seed_cells):
    dma = pltpu.SemaphoreType.DMA
    vmem = pltpu.VMEM
    x_first, x_second = swaps(lax.axis_size("gx"))
    y_first, y_second = swaps(lax.axis_size("gy"))
    flat = populations.reshape(19, N * N, NZ)
    seeds = seed_cells.reshape(1, SEEDS)

    xa, xb = pl.pallas_call(
        x_pack_kernel,
        out_shape=[shape(X_LEN, N, NZ)] * 2,
        in_specs=[VM] * 2,
        out_specs=[VM] * 2,
        compiler_params=params(),
        cost_estimate=cost(5_000_000, 1_500_000),
        name="x_pack",
    )(populations[:, :3], populations[:, N - 3 :])
    xb = lax.ppermute(xb, "gx", x_second)
    xa = lax.ppermute(xa, "gx", x_first)
    g_rows, hot_in, hot = pl.pallas_call(
        rows_kernel,
        out_shape=[
            shape(6, 19, N, NZ),
            jax.ShapeDtypeStruct(((N + 2) * N, 3 * SEEDS), BF16),
            jax.ShapeDtypeStruct((6 * WIDE, 3 * SEEDS), BF16),
        ],
        in_specs=[VM] * 2,
        out_specs=[VM] * 3,
        compiler_params=params(),
        cost_estimate=cost(5_000_000, 3_500_000),
        name="end_rows",
    )(flat, seeds)
    ya, yb, t = pl.pallas_call(
        y_pack_kernel,
        out_shape=[shape(Y_LEN, NZ), shape(FAR_LEN, NZ), shape(6, 19, T_LEN, NZ)],
        in_specs=[VM] * 3,
        out_specs=[VM] * 3,
        scratch_shapes=[
            vmem((X_LEN, N, NZ), F32),
            vmem((X_LEN, N, NZ), F32),
            vmem((2, N_A, T_LEN, NZ), F32),
        ],
        compiler_params=params(),
        cost_estimate=cost(5_000_000, 2_000_000),
        name="y_pack",
    )(g_rows, xb, xa)
    yb = lax.ppermute(yb, "gy", y_second)
    ya = lax.ppermute(ya, "gy", y_first)
    inside, fw, qw, pm, pick = pl.pallas_call(
        inside_kernel,
        out_shape=[
            shape(19, N, N, NZ),
            shape(2, 14, WIDE, NZ),
            shape(2, 4, WIDE, NZ),
            shape(4, 4, WIDE, NZ),
            shape(9, SEEDS),
        ],
        in_specs=[VM] * 6,
        out_specs=[VM] * 5,
        scratch_shapes=[
            vmem((19, N + 6, N, NZ), F32),
            vmem((19, N + 4, N, NZ), F32),
            vmem((4, (N + 2) * N, NZ), F32),
            vmem((3, (N + 2) * N, NZ), F32),
        ],
        compiler_params=params(),
        cost_estimate=cost(50_000_000, 30_000_000),
        name="inside",
    )(flat, t, xa, xb, hot_in, seeds)
    inside = inside.reshape(19, N, 2, 8, NZ)
    side_scratch = [
        vmem((PAD_LEN, NZ), F32),
        vmem((19, T_LEN, NZ), F32),
        vmem((N_A, T_LEN, NZ), F32),
        vmem((9, T_LEN, NZ), F32),
        vmem((N_A, WIDE, NZ), F32),
    ]
    half, pick = pl.pallas_call(
        first_side_kernel,
        out_shape=[shape(19, N, 2, 8, NZ), shape(9, SEEDS)],
        in_specs=[VM] * 8,
        out_specs=[ANY, VM],
        scratch_shapes=side_scratch + [vmem((19, N * 8, NZ), F32), dma((20,))],
        compiler_params=params(),
        cost_estimate=cost(5_000_000, 4_000_000),
        name="first_side",
    )(ya, inside, fw, qw, pm, pick, hot, seeds)
    out, grad, q_value, r_value, share = pl.pallas_call(
        second_side_kernel,
        out_shape=[shape(19, N, N, NZ), shape(9, 1, 1, SEEDS)] + [shape(1, 1, SEEDS)] * 3,
        in_specs=[VM] * 7 + [ANY],
        out_specs=[ANY] + [VM] * 4,
        scratch_shapes=side_scratch + [vmem((19, N, NZ), F32), dma((19,))],
        input_output_aliases={7: 0},
        compiler_params=params(),
        cost_estimate=cost(5_000_000, 3_000_000),
        name="second_side",
    )(yb, fw, qw, pm, pick, hot, seeds, half.reshape(19, N, N, NZ))
    return out, grad, q_value, r_value, share


def solution(mesh):
    in_specs = (P(None, "gx", "gy", None), P("gx", "gy", None))
    out_specs = (
        P(None, "gx", "gy", None),
        P(None, "gx", "gy", None),
        P("gx", "gy", None),
        P("gx", "gy", None),
        P("gx", "gy", None),
    )
    return jax.shard_map(
        per_device, mesh=mesh, in_specs=in_specs, out_specs=out_specs, check_vma=False
    )
```
